32 devices in a mesh: seq: 4 (over x, core), batch: 8 (over z, y).
Axes of the slice: x: 2, y: 2, z: 4, core: 2. Of those that a mesh axis runs over, the one named last changes fastest.
Arguments:
- values: bfloat16 [24, 512, 768], P('batch', 'seq'), may hold values from -6 to 6
- names: bfloat16 [24, 1536, 768], P('batch', 'seq'), may hold values from -6 to 6
- counts: int32 [24, 512], P('batch', 'seq'), may hold values from 0 to 20, as said below
- valid: int32 [24, 512], P('batch', 'seq'), may hold values from 0 to 1, as said below
- out_grad: bfloat16 [24, 512, 768], P('batch', 'seq'), may hold values from -6 to 6
- master: float32 [9984, 768], P(('seq', 'batch')), may hold values from -2 to 2
- momentum: float32 [9984, 768], P(('seq', 'batch')), may hold values from -0.0048828125 to 0.0048828125
- average: float32 [9984, 768], P(('seq', 'batch')), may hold values from -0.21875 to 0.21875
- vectors: float32 [9216], replicated, may hold values from -1 to 2.1
- vector_momentum: float32 [9216], replicated, may hold values from -0.0048828125 to 0.0048828125
- vector_average: float32 [9216], replicated, may hold values from -3 to 3
Outputs:
- output: bfloat16 [24, 512, 768], P('batch', 'seq')
- grad_values: float32 [24, 512, 768], P('batch', 'seq')
- grad_names: float32 [24, 1536, 768], P('batch', 'seq')
- grad_norm: float32 [], replicated
- new_master: float32 [9984, 768], P(('seq', 'batch'))
- new_momentum: float32 [9984, 768], P(('seq', 'batch'))
- new_average: float32 [9984, 768], P(('seq', 'batch'))
- new_weights: bfloat16 [9984, 768], P(('seq', 'batch'))
- new_vectors: float32 [9216], replicated
- new_vector_momentum: float32 [9216], replicated
- new_vector_average: float32 [9216], replicated
The draws below stay inside these ranges and needn't reach their ends.
Inputs may be any that keep to these rules, and one draw needn't show every extreme that they name: Positions with valid 0 have count 0. The counts of one row's 128 positions on one device add up to at most 384, and on every device some row reaches it in every draw. Each row is valid on a prefix of 128 positions or more; of the 3 rows of one device, one is valid throughout.
All inputs are finite; a program needn't handle non-finite values.
Results may differ from the reference program's by a relative error of at most 0.018.
The reference program's roundings to bfloat16 on the way count: a program that leaves them out, or rounds other values in their place, can miss the bound.
Values may be sent and summed in bfloat16 or wider, within the bound.
A program may use at most 128 MiB of HBM per device.

```python
import math
import jax
import jax.numpy as jnp
from jax import lax

D = 768
HEADS = 12
HEAD = 64
FF = 3072
MAX_NAMES = 20
LEN_DEV = 128
ROW_DEV = 3
NAME_DEV = 384
LENGTH = 512
ROWS = 24
NAMES = 1536
MAT_ROWS = 9984
VEC = 9216
N_SEQ = 4


def mask_and_counts(key):
    key_length, key_full, key_count = jax.random.split(key, 3)
    shard_total = LENGTH // LEN_DEV
    row_lengths = jax.random.randint(key_length, (ROWS,), LEN_DEV, LENGTH + 1)
    chosen = jax.random.randint(key_full, (ROWS // ROW_DEV,), 0, ROW_DEV)
    row_ids = jnp.arange(ROWS)
    is_full = row_ids % ROW_DEV == chosen[row_ids // ROW_DEV]
    row_lengths = jnp.where(is_full, LENGTH, row_lengths)
    positions = jnp.arange(LENGTH)
    valid_mask = (positions[None, :] < row_lengths[:, None]).astype(jnp.int32)
    raw_counts = MAX_NAMES // jax.random.randint(key_count, (ROWS, LENGTH), 1, MAX_NAMES + 1)
    raw_counts = jnp.where(is_full[:, None], jnp.maximum(raw_counts, NAME_DEV // LEN_DEV), raw_counts) * valid_mask
    shard_counts = raw_counts.reshape(ROWS, shard_total, LEN_DEV)
    before = jnp.cumsum(shard_counts, axis=2) - shard_counts
    capped = jnp.clip(NAME_DEV - before, 0, shard_counts)
    return (valid_mask, capped.reshape(ROWS, LENGTH).astype(jnp.int32))


def draw_counts(key, part):
    return mask_and_counts(key)[1]


def draw_valid(key, part):
    return mask_and_counts(key)[0]


def draw_master(key, part):
    key = jax.random.fold_in(key, 5)
    row_index = jnp.arange(MAT_ROWS)[:, None]
    base = D ** (-0.5)
    scales = jnp.where(row_index < 3 * D, base, jnp.where(row_index < 4 * D, 4.0 * base, jnp.where(row_index < 5 * D, 1.5 * base, jnp.where(row_index < 5 * D + FF, base, FF ** (-0.5)))))
    normal_draw = jnp.clip(jax.random.normal(key, (MAT_ROWS, D), jnp.float32), -3.0, 3.0)
    return normal_draw * scales


def draw_vectors(key, part):
    key = jax.random.fold_in(key, 7)
    key_bias, key_gain = jax.random.split(key)
    entry_index = jnp.arange(VEC)
    bias_values = 0.3 * jnp.clip(jax.random.normal(key_bias, (VEC,), jnp.float32), -3.0, 3.0)
    gain_values = jnp.exp(jax.random.uniform(key_gain, (VEC,), jnp.float32, -0.7, 0.7))
    is_gain = (entry_index >= 3 * D) & (entry_index < 4 * D) | (entry_index >= 6 * D) & (entry_index < 7 * D)
    return jnp.where(is_gain, gain_values, bias_values)


def shard_levels(key, dims, cuts, low, high):
    level = 1.0
    for position, blocks in cuts:
        steps = jax.random.uniform(jax.random.fold_in(jax.random.fold_in(key, 6), position), (blocks,), jnp.float32, low / len(cuts), high / len(cuts))
        level = level * jnp.repeat(jnp.exp(steps), dims[position] // blocks).reshape((-1,) + (1,) * (len(dims) - 1 - position))
    return level


def bell_draw(key, shape, scale, most, cuts=(), held_as=jnp.bfloat16):
    values = scale * jax.random.normal(key, shape, jnp.float32)
    if cuts:
        values = values * shard_levels(key, shape, cuts, -0.22, 0.18)
    return jnp.clip(values, -most, most).astype(held_as)


def setup_inputs(seed: int = 0) -> dict:
    arg_keys = jax.random.split(jax.random.key(seed), 12)
    return {
        "values": bell_draw(arg_keys[0], (ROWS, LENGTH, D), 1.0, 6.0, ((0, 8), (1, 4))),
        "names": bell_draw(arg_keys[1], (ROWS, NAMES, D), 1.0, 6.0, ((0, 8), (1, 4))),
        "counts": draw_counts(jax.random.fold_in(arg_keys[11], 71), 0),
        "valid": draw_valid(jax.random.fold_in(arg_keys[11], 71), 0),
        "out_grad": bell_draw(arg_keys[4], (ROWS, LENGTH, D), 1.0, 6.0, ((0, 8), (1, 4))),
        "master": draw_master(jax.random.fold_in(arg_keys[11], 71), 0),
        "momentum": bell_draw(arg_keys[6], (MAT_ROWS, D), ((MAT_ROWS * D + VEC) ** -0.5), 0.0048828125, ((0, 32),), jnp.float32),
        "average": bell_draw(arg_keys[7], (MAT_ROWS, D), D ** -0.5, 0.21875, ((0, 32),), jnp.float32),
        "vectors": draw_vectors(jax.random.fold_in(arg_keys[11], 71), 0),
        "vector_momentum": bell_draw(arg_keys[9], (VEC,), ((MAT_ROWS * D + VEC) ** -0.5), 0.0048828125, (), jnp.float32),
        "vector_average": bell_draw(arg_keys[10], (VEC,), 0.5, 3.0, (), jnp.float32),
    }


@jax.custom_vjp
def low(v):
    return lax.optimization_barrier(v.astype(jnp.bfloat16)).astype(jnp.float32)

@jax.custom_vjp
def low_back(v):
    return v

def low_keep(v):
    return (low(v), None)

def low_pass(kept, grad):
    return (grad,)

def back_keep(v):
    return (v, None)

def back_low(kept, grad):
    return (low(grad),)
low.defvjp(low_keep, low_pass)
low_back.defvjp(back_keep, back_low)
HIGH = lax.Precision.HIGHEST
norm_eps = 1e-05
step_rate = 40.0
vector_rate = 240.0
momentum_decay = 0.5
average_decay = 0.5

def layer_norm(value_in, gain, shift):
    centre = lax.optimization_barrier(jnp.mean(value_in, axis=-1, keepdims=True))
    centred = value_in - centre
    spread = lax.optimization_barrier(jnp.mean(centred * centred, axis=-1, keepdims=True))
    return centred * lax.rsqrt(spread + norm_eps) * gain + shift

def members(shard_counts):
    slot_ends = jnp.cumsum(shard_counts, axis=-1)
    slot_starts = slot_ends - shard_counts
    slot_ids = jnp.arange(NAME_DEV, dtype=jnp.int32)
    inside = (slot_ids >= slot_starts[..., None]) & (slot_ids < slot_ends[..., None])
    return inside.astype(jnp.float32)

def row_attention(pieces):
    query_row, key_row, value_row, valid_row = pieces
    query_heads = query_row.reshape(LENGTH, HEADS, HEAD)
    key_heads = key_row.reshape(LENGTH, HEADS, HEAD)
    value_heads = value_row.reshape(LENGTH, HEADS, HEAD)
    scores = low_back(jnp.einsum('qhd,khd->hqk', query_heads, key_heads, precision=HIGH) * HEAD ** (-0.5))
    scores = jnp.where(valid_row[None, None, :] > 0, scores, -1e+30)
    top_score = lax.optimization_barrier(jnp.max(scores, axis=-1, keepdims=True))
    exp_scores = jnp.exp(scores - top_score)
    prob = exp_scores / lax.optimization_barrier(jnp.sum(exp_scores, axis=-1, keepdims=True))
    context = jnp.einsum('hqk,khd->qhd', low(prob), value_heads, precision=HIGH)
    return context.reshape(LENGTH, D)

def group_forward(weights, vectors, values, names, counts, valid):
    row_count = values.shape[0]
    token_count = row_count * LENGTH
    w_qkv = weights[0:3 * D]
    w_attn = weights[3 * D:4 * D]
    w_unite = weights[4 * D:5 * D]
    w_in = weights[5 * D:5 * D + FF]
    w_down = weights[5 * D + FF:5 * D + 2 * FF]
    bias_q = vectors[0:D]
    bias_v = vectors[D:2 * D]
    bias_o = vectors[2 * D:3 * D]
    gain_one = vectors[3 * D:4 * D]
    shift_one = vectors[4 * D:5 * D]
    bias_down = vectors[5 * D:6 * D]
    gain_two = vectors[6 * D:7 * D]
    shift_two = vectors[7 * D:8 * D]
    bias_in = vectors[8 * D:8 * D + FF]
    shard_counts = counts.reshape(row_count, N_SEQ, LEN_DEV)
    inside = members(shard_counts)
    summed = jnp.einsum('rstn,rsnd->rstd', inside, names.reshape(row_count, N_SEQ, NAME_DEV, D), precision=HIGH)
    divisor = jnp.maximum(shard_counts.astype(jnp.float32), 1.0)[..., None]
    pooled = low(low_back(summed / divisor)).reshape(token_count, D)
    united = values.reshape(token_count, D) + low_back(jnp.dot(pooled, w_unite, precision=HIGH))
    first = low(united)
    projected = jnp.dot(first, w_qkv.T, precision=HIGH)
    query = low(low_back(projected[:, 0:D] + bias_q))
    key_proj = low(low_back(projected[:, D:2 * D]))
    value_proj = low(low_back(projected[:, 2 * D:3 * D] + bias_v))
    attend = jax.checkpoint(row_attention)
    context = lax.map(attend, (query.reshape(row_count, LENGTH, D), key_proj.reshape(row_count, LENGTH, D), value_proj.reshape(row_count, LENGTH, D), valid))
    context = low(low_back(context.reshape(token_count, D)))
    attn_out = low_back(jnp.dot(context, w_attn, precision=HIGH) + bias_o)
    normed = layer_norm(united + attn_out, gain_one, shift_one)
    up_proj = low_back(jnp.dot(low(normed), w_in.T, precision=HIGH) + bias_in)
    hidden = low(jax.nn.gelu(up_proj, approximate=False))
    down_proj = low_back(jnp.dot(hidden, w_down, precision=HIGH) + bias_down)
    result = layer_norm(normed + down_proj, gain_two, shift_two)
    return result.reshape(row_count, LENGTH, D)

def apply_update(weight, moment, mean_state, gradient, clip_factor, rate):
    clipped = gradient * clip_factor
    new_moment = momentum_decay * moment + clipped
    new_weight = weight - rate * (clipped + momentum_decay * new_moment)
    new_mean = average_decay * mean_state + (1.0 - average_decay) * new_weight
    return (new_weight, new_moment, new_mean)

def reference(values, names, counts, valid, out_grad, master, momentum, average, vectors, vector_momentum, vector_average):
    group_rows = math.gcd(ROWS, 8)
    group_count = ROWS // group_rows

    def split_rows(array_in):
        return array_in.reshape((group_count, group_rows) + array_in.shape[1:])
    counts_split = split_rows(counts)
    valid_split = split_rows(valid)
    cotangent = split_rows(out_grad.astype(jnp.float32))

    def whole(master_in, vectors_in, values_in, names_in):
        rounded = low(master_in)

        def one_group(carry, pieces):
            return (carry, jax.checkpoint(group_forward)(rounded, vectors_in, pieces[0], pieces[1], pieces[2], pieces[3]))
        carry_out, results = lax.scan(one_group, jnp.zeros((), jnp.float32), (values_in, names_in, counts_split, valid_split))
        return results
    result, pullback = jax.vjp(whole, master, vectors, split_rows(values.astype(jnp.float32)), split_rows(names.astype(jnp.float32)))
    grad_master, grad_vectors, grad_values, grad_names = pullback(cotangent)
    squares = jnp.sum(grad_master * grad_master) + jnp.sum(grad_vectors * grad_vectors)
    grad_norm = jnp.sqrt(squares)
    clip_factor = 1.0 / jnp.maximum(grad_norm, 1.0)
    new_master, new_momentum, new_average = apply_update(master, momentum, average, grad_master, clip_factor, step_rate)
    new_vectors, new_vector_momentum, new_vector_average = apply_update(vectors, vector_momentum, vector_average, grad_vectors, clip_factor, vector_rate)
    return (result.reshape(ROWS, LENGTH, D).astype(jnp.bfloat16), grad_values.reshape(ROWS, LENGTH, D), grad_names.reshape(ROWS, NAMES, D), grad_norm, new_master, new_momentum, new_average, new_master.astype(jnp.bfloat16), new_vectors, new_vector_momentum, new_vector_average)
```

```python
import functools
import math

import jax
import jax.numpy as jnp
from jax import lax
from jax.experimental import pallas as pl
from jax.experimental.pallas import tpu as pltpu
from jax.sharding import PartitionSpec as P

MESH = pl.DeviceIdType.MESH

D = 768
HEAD = 64
FF = 3072
NAME_DEV = 384


norm_eps = 1e-05
step_rate = 40.0
vector_rate = 240.0
momentum_decay = 0.5
average_decay = 0.5
big_negative = -1e30


def layer_norm(value_in, gain, shift):
    centre = jnp.mean(value_in, axis=-1, keepdims=True)
    centred = value_in - centre
    spread = jnp.mean(centred * centred, axis=-1, keepdims=True)
    return centred * lax.rsqrt(spread + norm_eps) * gain + shift


def exact_gelu(value_in):
    return jax.nn.gelu(value_in, approximate=False)


def matmul(first_op, second_op):
    return jnp.dot(first_op, second_op, preferred_element_type=jnp.float32)


def matmul_t(first_op, second_op):
    return lax.dot_general(
        first_op, second_op, (((1,), (1,)), ((), ())), preferred_element_type=jnp.float32
    )


def tokens_t(first_op, second_op):
    return lax.dot_general(
        first_op, second_op, (((0,), (0,)), ((), ())), preferred_element_type=jnp.float32
    )


def split_heads(array_in):
    return array_in.reshape(array_in.shape[0], array_in.shape[1], array_in.shape[2] // HEAD, HEAD)


def block_scores(query_part, key_part, mask_part):
    scores = jnp.einsum(
        "bqhd,bkhd->bhqk",
        split_heads(query_part),
        split_heads(key_part),
        preferred_element_type=jnp.float32,
    ) * HEAD ** (-0.5)
    return jnp.where(mask_part[:, None, None, :] > 0, scores, big_negative)


def attend_block(pieces):
    query_part, key_part, value_part, mask_part = pieces
    scores = block_scores(query_part, key_part, mask_part)
    top_score = jnp.max(scores, axis=-1, keepdims=True)
    exp_scores = jnp.exp(scores - top_score)
    exp_total = jnp.sum(exp_scores, axis=-1, keepdims=True)
    prob = (exp_scores / exp_total).astype(jnp.bfloat16)
    context = jnp.einsum(
        "bhqk,bkhd->bqhd", prob, split_heads(value_part), preferred_element_type=jnp.float32
    )
    log_total = (top_score + jnp.log(exp_total))[..., 0]
    return (context.reshape(query_part.shape).astype(jnp.bfloat16), log_total)


def attend_back(pieces):
    query_part, key_part, value_part, mask_part, log_total, grad_context = pieces
    scores = block_scores(query_part, key_part, mask_part)
    prob = jnp.exp(scores - log_total[..., None])
    grad_heads = split_heads(grad_context)
    grad_prob = jnp.einsum(
        "bqhd,bkhd->bhqk", grad_heads, split_heads(value_part), preferred_element_type=jnp.float32
    )
    grad_value = jnp.einsum(
        "bhqk,bqhd->bkhd", prob.astype(jnp.bfloat16), grad_heads, preferred_element_type=jnp.float32
    )
    inner = jnp.sum(grad_prob * prob, axis=-1, keepdims=True)
    grad_scores = (prob * (grad_prob - inner)).astype(jnp.bfloat16)
    scale = HEAD ** (-0.5)
    grad_query = (
        jnp.einsum(
            "bhqk,bkhd->bqhd",
            grad_scores,
            split_heads(key_part),
            preferred_element_type=jnp.float32,
        )
        * scale
    )
    grad_key = (
        jnp.einsum(
            "bhqk,bqhd->bkhd",
            grad_scores,
            split_heads(query_part),
            preferred_element_type=jnp.float32,
        )
        * scale
    )
    return (
        grad_query.reshape(query_part.shape),
        grad_key.reshape(key_part.shape),
        grad_value.reshape(value_part.shape),
    )


def apply_update(weight, moment, mean_state, gradient, clip_factor, rate):
    clipped = gradient * clip_factor
    new_moment = momentum_decay * moment + clipped
    new_weight = weight - rate * (clipped + momentum_decay * new_moment)
    new_mean = average_decay * mean_state + (1.0 - average_decay) * new_weight
    return (new_weight, new_moment, new_mean)


def place():
    s=lax.axis_index("seq"); b=lax.axis_index("batch")
    return s//2, s%2, b//2, b%2
def when(cond,fn):
    if cond is None or cond is True: fn()
    elif cond is False: pass
    else: pl.when(cond)(fn)

class Gather:
    cols=((0,512),(512,256))
    def __init__(self,w,stage,send_sem,recv_sem,sib_sem):
        self.w=w; self.stage=stage; self.ss=send_sem; self.rs=recv_sem; self.bs=sib_sem
        self.x,self.c,self.z,self.y=place()
        self.sent=[]
    def dev(self,d):
        x,c,z,y=self.x,self.c,self.z,self.y
        return {"x":{"seq":(1-x)*2+c,"batch":z*2+y},"y":{"seq":x*2+c,"batch":z*2+1-y},"c":{"seq":x*2+1-c,"batch":z*2+y},
                "u":{"seq":x*2+c,"batch":jnp.minimum(z+1,3)*2+y},"d":{"seq":x*2+c,"batch":jnp.maximum(z-1,0)*2+y}}[d]
    def region(self,t,x0,z0,y0,n,c=None):
        c=self.c if c is None else c
        off=pl.multiple_of((2*x0+c)*2496+z0*624+320*y0,16)
        c0,cn=self.cols[t]
        return self.w.at[pl.ds(off,n),pl.ds(c0,cn)]
    def both(self,y0,cond,fn):
        if isinstance(y0,int):
            when(cond,lambda: fn(320 if y0==0 else 304))
        else:
            c0=(y0==0); c1=(y0==1)
            if cond is not None: c0=jnp.logical_and(c0,cond); c1=jnp.logical_and(c1,cond)
            pl.when(c0)(lambda: fn(320)); pl.when(c1)(lambda: fn(304))
    def copy(self,t,x0,z0,y0,d,n,own):
        c0,cn=self.cols[t]
        dst=self.region(t,x0,z0,y0,n)
        src=self.stage.at[pl.ds(0,n),pl.ds(c0,cn)] if own else dst
        k=x0*8+z0*2+y0
        i={"u":0,"d":1,"x":2,"y":2,"c":3}[d]
        if d in "xy" and ((t==0)!=(d=="y")): i=4
        rsem=self.bs.at[t,k] if d=="c" else self.rs.at[t,k]
        return pltpu.make_async_remote_copy(src_ref=src,dst_ref=dst,send_sem=self.ss.at[t,k,i],recv_sem=rsem,device_id=self.dev(d),device_id_type=MESH)
    def send(self,t,x0,z0,y0,dirs,own=False,cond=None):
        for d,dc in dirs:
            cc=cond if dc is None else (dc if cond is None else jnp.logical_and(cond,dc))
            self.both(y0,cc,lambda n,d=d: self.copy(t,x0,z0,y0,d,n,own).start())
            self.sent.append((t,x0,z0,y0,d,own,cc))
    def recv(self,t,x0,z0,y0,cond=None):
        self.both(y0,cond,lambda n: self.copy(t,x0,z0,y0,"x",n,False).wait_recv())
    def recv_sib(self,t,x0,z0,y0):
        def f(n):
            r=self.region(t,x0,z0,y0,n,c=1-self.c)
            k=x0*8+z0*2+y0
            pltpu.make_async_remote_copy(src_ref=r,dst_ref=r,send_sem=self.ss.at[t,k,0],recv_sem=self.bs.at[t,k],device_id=self.dev("c"),device_id_type=MESH).wait_recv()
        self.both(y0,None,f)
    def events(self):
        x,c,z,y=self.x,self.c,self.z,self.y
        up=z<3; dn=z>0
        ev=[]
        def start():
            self.send(0,x,z,y,[("x",None),("u",up),("d",dn),("y",None),("c",None)],own=True)
            self.send(1,x,z,y,[("y",None),("u",up),("d",dn),("x",None),("c",None)],own=True)
        ev.append(start)
        def first():
            self.recv(0,1-x,z,y); self.send(0,1-x,z,y,[("u",up),("d",dn),("y",None),("c",None)])
            self.recv(1,x,z,1-y); self.send(1,x,z,1-y,[("u",up),("d",dn),("x",None),("c",None)])
        ev.append(first)
        for d in (1,2,3):
            for j in (0,1):
                def zstep(d=d,j=j):
                    for t in (0,1):
                        for sgn in (-1,1):
                            z0=z+sgn*d
                            ok=(z0>=0) if sgn<0 else (z0<=3)
                            x0,y0=(x if j==0 else 1-x, y) if t==0 else (x, y if j==0 else 1-y)
                            self.recv(t,x0,z0,y0,cond=ok)
                            relay=[("u",up)] if sgn<0 else [("d",dn)]
                            self.send(t,x0,z0,y0,relay+[("y" if t==0 else "x",None),("c",None)],cond=ok)
                ev.append(zstep)
        for z0 in range(4):
            for j in (0,1):
                def leaf(z0=z0,j=j):
                    self.recv(0,j,z0,1-y); self.send(0,j,z0,1-y,[("c",None)])
                    self.recv(1,1-x,z0,j); self.send(1,1-x,z0,j,[("c",None)])
                ev.append(leaf)
        return ev
    def finish(self):
        for t in (0,1):
            for x0 in (0,1):
                for z0 in range(4):
                    for y0 in (0,1):
                        self.recv_sib(t,x0,z0,y0)
        for t,x0,z0,y0,d,own,cc in self.sent:
            self.both(y0,cc,lambda n: self.copy(t,x0,z0,y0,d,n,own).wait_send())

def barrier(g):
    bar=pltpu.get_barrier_semaphore()
    x,c,z,y=g.x,g.c,g.z,g.y
    for d,cond in (("x",None),("y",None),("c",None),("u",z<3),("d",z>0)):
        when(cond,lambda d=d: pl.semaphore_signal(bar,1,device_id=g.dev(d),device_id_type=MESH))
    pl.semaphore_wait(bar,3+(z<3).astype(jnp.int32)+(z>0).astype(jnp.int32))

def ag_kernel(master,w,stage,edge,edge_sem,send_sem,recv_sem,sib_sem,own_sem):
    g=Gather(w,stage,send_sem,recv_sem,sib_sem)
    x,c,z,y=g.x,g.c,g.z,g.y
    barrier(g)
    ecopy=pltpu.make_async_remote_copy(src_ref=master.at[pl.ds(0,8)],dst_ref=edge,send_sem=edge_sem.at[0],recv_sem=edge_sem.at[1],device_id=g.dev("y"),device_id_type=MESH)
    @pl.when(y==1)
    def _():
        ecopy.start()
        stage[0:304]=master[8:312].astype(jnp.bfloat16)
        stage[304:320]=jnp.zeros((16,768),jnp.bfloat16)
    @pl.when(y==0)
    def _():
        stage[0:304]=master[0:304].astype(jnp.bfloat16)
        ecopy.wait_recv()
        stage[304:320]=jnp.concatenate([master[304:312],edge[...]],axis=0).astype(jnp.bfloat16)
    def own(n):
        off=pl.multiple_of((2*x+c)*2496+z*624+320*y,16)
        return pltpu.make_async_copy(stage.at[pl.ds(0,n)],w.at[pl.ds(off,n)],own_sem)
    g.both(y,None,lambda n: own(n).start())
    for e in g.events(): e()
    g.finish()
    g.both(y,None,lambda n: own(n).wait())
    pl.when(y==1)(lambda: ecopy.wait_send())

def gather_weights(master):
    return pl.pallas_call(ag_kernel,out_shape=jax.ShapeDtypeStruct((9984,768),jnp.bfloat16),
        in_specs=[pl.BlockSpec(memory_space=pltpu.VMEM)],out_specs=pl.BlockSpec(memory_space=pl.ANY),
        scratch_shapes=[pltpu.VMEM((320,768),jnp.bfloat16),pltpu.VMEM((8,768),jnp.float32),pltpu.SemaphoreType.DMA((2,)),
            pltpu.SemaphoreType.DMA((2,16,5)),pltpu.SemaphoreType.DMA((2,16)),pltpu.SemaphoreType.DMA((2,16)),pltpu.SemaphoreType.DMA],
        compiler_params=pltpu.CompilerParams(collective_id=0,has_side_effects=True,vmem_limit_bytes=40<<20),name="gather_weights")(master)


def local(
    tuned,
    values,
    names,
    counts,
    valid,
    out_grad,
    master,
    momentum,
    average,
    vectors,
    vector_momentum,
    vector_average,
):
    row_count, row_span, width = values.shape
    token_count = row_count * row_span
    if tuned:
        weights = gather_weights(master)
    else:
        weights = lax.all_gather(master.astype(jnp.bfloat16), ("seq", "batch"), axis=0, tiled=True)
    w_qkv = weights[0 : 3 * D]
    w_attn = weights[3 * D : 4 * D]
    w_unite = weights[4 * D : 5 * D]
    w_in = weights[5 * D : 5 * D + FF]
    w_down = weights[5 * D + FF : 5 * D + 2 * FF]
    bias_q = vectors[0:D]
    bias_v = vectors[D : 2 * D]
    bias_o = vectors[2 * D : 3 * D]
    gain_one = vectors[3 * D : 4 * D]
    shift_one = vectors[4 * D : 5 * D]
    bias_down = vectors[5 * D : 6 * D]
    gain_two = vectors[6 * D : 7 * D]
    shift_two = vectors[7 * D : 8 * D]
    bias_in = vectors[8 * D : 8 * D + FF]
    slot_ends = jnp.cumsum(counts, axis=1)
    slot_starts = slot_ends - counts
    slot_ids = jnp.arange(NAME_DEV, dtype=jnp.int32)
    inside = (slot_ids >= slot_starts[:, :, None]) & (slot_ids < slot_ends[:, :, None])
    summed = jnp.einsum(
        "rtn,rnd->rtd", inside.astype(jnp.bfloat16), names, preferred_element_type=jnp.float32
    )
    divisor = jnp.maximum(counts.astype(jnp.float32), 1.0)[:, :, None]
    pooled = (summed / divisor).astype(jnp.bfloat16).reshape(token_count, D)
    united = values.reshape(token_count, D).astype(jnp.float32) + matmul(pooled, w_unite)
    first = united.astype(jnp.bfloat16)
    projected = matmul_t(first, w_qkv)
    query = (projected[:, 0:D] + bias_q).astype(jnp.bfloat16).reshape(row_count, row_span, D)
    key_proj = projected[:, D : 2 * D].astype(jnp.bfloat16).reshape(row_count, row_span, D)
    value_proj = (
        (projected[:, 2 * D : 3 * D] + bias_v).astype(jnp.bfloat16).reshape(row_count, row_span, D)
    )
    key_all, value_all, mask_all = (
        lax.all_gather(key_proj, "seq", axis=1, tiled=True),
        lax.all_gather(value_proj, "seq", axis=1, tiled=True),
        lax.all_gather(valid.astype(jnp.bfloat16), "seq", axis=1, tiled=True),
    )
    block_rows = math.gcd(row_count, max(1, 512 // row_span))
    block_count = row_count // block_rows

    def blocked(array_in):
        return array_in.reshape((block_count, block_rows) + array_in.shape[1:])

    context, log_total = lax.map(
        attend_block, (blocked(query), blocked(key_all), blocked(value_all), blocked(mask_all))
    )
    context = context.reshape(token_count, D)
    attn_out = matmul(context, w_attn) + bias_o
    normed, norm_one_back = jax.vjp(layer_norm, united + attn_out, gain_one, shift_one)
    lowered = normed.astype(jnp.bfloat16)
    up_proj = matmul_t(lowered, w_in) + bias_in
    activated, gelu_back = jax.vjp(exact_gelu, up_proj)
    hidden = activated.astype(jnp.bfloat16)
    down_proj = matmul(hidden, w_down) + bias_down
    result, norm_two_back = jax.vjp(layer_norm, normed + down_proj, gain_two, shift_two)
    output = result.astype(jnp.bfloat16).reshape(row_count, row_span, D)
    grad_two, grad_gain_two, grad_shift_two = norm_two_back(
        out_grad.reshape(token_count, D).astype(jnp.float32)
    )
    grad_down = grad_two.astype(jnp.bfloat16)
    grad_bias_down = jnp.sum(grad_down.astype(jnp.float32), axis=0)
    grad_w_down = tokens_t(hidden, grad_down)
    grad_hidden = matmul_t(grad_down, w_down)
    grad_up = gelu_back(grad_hidden)[0].astype(jnp.bfloat16)
    grad_bias_in = jnp.sum(grad_up.astype(jnp.float32), axis=0)
    grad_w_in = tokens_t(grad_up, lowered)
    grad_one, grad_gain_one, grad_shift_one = norm_one_back(grad_two + matmul(grad_up, w_in))
    grad_attn = grad_one.astype(jnp.bfloat16)
    grad_bias_o = jnp.sum(grad_attn.astype(jnp.float32), axis=0)
    grad_w_attn = tokens_t(context, grad_attn)
    grad_context = matmul_t(grad_attn, w_attn).astype(jnp.bfloat16).reshape(row_count, row_span, D)
    grad_query, key_terms, value_terms = lax.map(
        attend_back,
        (
            blocked(query),
            blocked(key_all),
            blocked(value_all),
            blocked(mask_all),
            log_total,
            blocked(grad_context),
        ),
    )
    grad_key, grad_value = (
        lax.psum_scatter(
            key_terms.reshape(row_count, -1, D).astype(jnp.bfloat16),
            "seq",
            scatter_dimension=1,
            tiled=True,
        ).astype(jnp.float32),
        lax.psum_scatter(
            value_terms.reshape(row_count, -1, D).astype(jnp.bfloat16),
            "seq",
            scatter_dimension=1,
            tiled=True,
        ).astype(jnp.float32),
    )
    grad_q = grad_query.reshape(token_count, D).astype(jnp.bfloat16)
    grad_k = grad_key.reshape(token_count, D).astype(jnp.bfloat16)
    grad_v = grad_value.reshape(token_count, D).astype(jnp.bfloat16)
    grad_bias_q = jnp.sum(grad_q.astype(jnp.float32), axis=0)
    grad_bias_v = jnp.sum(grad_v.astype(jnp.float32), axis=0)
    grad_qkv = jnp.concatenate([grad_q, grad_k, grad_v], axis=1)
    grad_w_qkv = tokens_t(grad_qkv, first)
    grad_united = grad_one + matmul(grad_qkv, w_qkv)
    grad_unite = grad_united.astype(jnp.bfloat16)
    grad_w_unite = tokens_t(pooled, grad_unite)
    grad_pooled = lax.optimization_barrier(
        matmul_t(grad_unite, w_unite).astype(jnp.bfloat16)
    ).astype(jnp.float32)
    grad_pooled = grad_pooled.reshape(row_count, row_span, D) / divisor
    grad_names = jnp.einsum(
        "rtn,rtd->rnd", inside.astype(jnp.float32), grad_pooled, precision=lax.Precision.HIGHEST
    )
    grad_values = grad_united.reshape(row_count, row_span, D)
    vector_grads = jnp.concatenate(
        [
            grad_bias_q,
            grad_bias_v,
            grad_bias_o,
            grad_gain_one,
            grad_shift_one,
            grad_bias_down,
            grad_gain_two,
            grad_shift_two,
            grad_bias_in,
        ]
    )
    grads = jnp.concatenate([grad_w_qkv, grad_w_attn, grad_w_unite, grad_w_in, grad_w_down], axis=0)
    owned = lax.psum_scatter(grads.astype(jnp.bfloat16), ("seq", "batch"), scatter_dimension=0, tiled=True).astype(jnp.float32)
    local_squares = jnp.sum(owned * owned)
    vector_total, matrix_squares = lax.psum((vector_grads, local_squares), ("seq", "batch"))
    grad_norm = jnp.sqrt(matrix_squares + jnp.sum(vector_total * vector_total))
    clip_factor = 1.0 / jnp.maximum(grad_norm, 1.0)
    new_master, new_momentum, new_average = apply_update(
        master, momentum, average, owned, clip_factor, step_rate
    )
    new_vectors, new_vector_momentum, new_vector_average = apply_update(
        vectors, vector_momentum, vector_average, vector_total, clip_factor, vector_rate
    )
    return (
        output,
        grad_values,
        grad_names,
        grad_norm,
        new_master,
        new_momentum,
        new_average,
        new_master.astype(jnp.bfloat16),
        new_vectors,
        new_vector_momentum,
        new_vector_average,
    )


def solution(mesh):
    tuned = dict(mesh.shape) == {"seq": 4, "batch": 8}
    return jax.shard_map(
        functools.partial(local, tuned),
        mesh=mesh,
        in_specs=(
            P("batch", "seq", None),
            P("batch", "seq", None),
            P("batch", "seq"),
            P("batch", "seq"),
            P("batch", "seq", None),
            P(("seq", "batch"), None),
            P(("seq", "batch"), None),
            P(("seq", "batch"), None),
            P(),
            P(),
            P(),
        ),
        out_specs=(
            P("batch", "seq", None),
            P("batch", "seq", None),
            P("batch", "seq", None),
            P(),
            P(("seq", "batch"), None),
            P(("seq", "batch"), None),
            P(("seq", "batch"), None),
            P(("seq", "batch"), None),
            P(),
            P(),
            P(),
        ),
        check_vma=False,
    )
```

```python
import functools
import math

import jax
import jax.numpy as jnp
from jax import lax
from jax.experimental import pallas as pl
from jax.experimental.pallas import tpu as pltpu
from jax.sharding import PartitionSpec as P

MESH = pl.DeviceIdType.MESH

D = 768
HEAD = 64
FF = 3072
NAME_DEV = 384


norm_eps = 1e-05
step_rate = 40.0
vector_rate = 240.0
momentum_decay = 0.5
average_decay = 0.5
big_negative = -1e30


def layer_norm(value_in, gain, shift):
    centre = jnp.mean(value_in, axis=-1, keepdims=True)
    centred = value_in - centre
    spread = jnp.mean(centred * centred, axis=-1, keepdims=True)
    return centred * lax.rsqrt(spread + norm_eps) * gain + shift


def exact_gelu(value_in):
    return jax.nn.gelu(value_in, approximate=False)


def matmul(first_op, second_op):
    return jnp.dot(first_op, second_op, preferred_element_type=jnp.float32)


def matmul_t(first_op, second_op):
    return lax.dot_general(
        first_op, second_op, (((1,), (1,)), ((), ())), preferred_element_type=jnp.float32
    )


def tokens_t(first_op, second_op):
    return lax.dot_general(
        first_op, second_op, (((0,), (0,)), ((), ())), preferred_element_type=jnp.float32
    )


def split_heads(array_in):
    return array_in.reshape(array_in.shape[0], array_in.shape[1], array_in.shape[2] // HEAD, HEAD)


def block_scores(query_part, key_part, mask_part):
    scores = jnp.einsum(
        "bqhd,bkhd->bhqk",
        split_heads(query_part),
        split_heads(key_part),
        preferred_element_type=jnp.float32,
    ) * HEAD ** (-0.5)
    return jnp.where(mask_part[:, None, None, :] > 0, scores, big_negative)


def attend_block(pieces):
    query_part, key_part, value_part, mask_part = pieces
    scores = block_scores(query_part, key_part, mask_part)
    top_score = jnp.max(scores, axis=-1, keepdims=True)
    exp_scores = jnp.exp(scores - top_score)
    exp_total = jnp.sum(exp_scores, axis=-1, keepdims=True)
    prob = (exp_scores / exp_total).astype(jnp.bfloat16)
    context = jnp.einsum(
        "bhqk,bkhd->bqhd", prob, split_heads(value_part), preferred_element_type=jnp.float32
    )
    log_total = (top_score + jnp.log(exp_total))[..., 0]
    return (context.reshape(query_part.shape).astype(jnp.bfloat16), log_total)


def attend_back(pieces):
    query_part, key_part, value_part, mask_part, log_total, grad_context = pieces
    scores = block_scores(query_part, key_part, mask_part)
    prob = jnp.exp(scores - log_total[..., None])
    grad_heads = split_heads(grad_context)
    grad_prob = jnp.einsum(
        "bqhd,bkhd->bhqk", grad_heads, split_heads(value_part), preferred_element_type=jnp.float32
    )
    grad_value = jnp.einsum(
        "bhqk,bqhd->bkhd", prob.astype(jnp.bfloat16), grad_heads, preferred_element_type=jnp.float32
    )
    inner = jnp.sum(grad_prob * prob, axis=-1, keepdims=True)
    grad_scores = (prob * (grad_prob - inner)).astype(jnp.bfloat16)
    scale = HEAD ** (-0.5)
    grad_query = (
        jnp.einsum(
            "bhqk,bkhd->bqhd",
            grad_scores,
            split_heads(key_part),
            preferred_element_type=jnp.float32,
        )
        * scale
    )
    grad_key = (
        jnp.einsum(
            "bhqk,bqhd->bkhd",
            grad_scores,
            split_heads(query_part),
            preferred_element_type=jnp.float32,
        )
        * scale
    )
    return (
        grad_query.reshape(query_part.shape),
        grad_key.reshape(key_part.shape),
        grad_value.reshape(value_part.shape),
    )


def apply_update(weight, moment, mean_state, gradient, clip_factor, rate):
    clipped = gradient * clip_factor
    new_moment = momentum_decay * moment + clipped
    new_weight = weight - rate * (clipped + momentum_decay * new_moment)
    new_mean = average_decay * mean_state + (1.0 - average_decay) * new_weight
    return (new_weight, new_moment, new_mean)


def place():
    s = lax.axis_index("seq")
    b = lax.axis_index("batch")
    return s // 2, s % 2, b // 2, b % 2


def when(cond, fn):
    if cond is None:
        fn()
    else:
        pl.when(cond)(fn)


def both_of(first, second):
    if first is None:
        return second
    if second is None:
        return first
    return jnp.logical_and(first, second)


def by_size(y0, cond, fn):
    if isinstance(y0, int):
        when(cond, lambda: fn(320 if y0 == 0 else 304))
    else:
        when(both_of(y0 == 0, cond), lambda: fn(320))
        when(both_of(y0 == 1, cond), lambda: fn(304))


def neighbour(d):
    x, c, z, y = place()
    if d == "x":
        return {"seq": (1 - x) * 2 + c, "batch": z * 2 + y}
    if d == "y":
        return {"seq": x * 2 + c, "batch": z * 2 + 1 - y}
    if d == "c":
        return {"seq": x * 2 + 1 - c, "batch": z * 2 + y}
    if d == "u":
        return {"seq": x * 2 + c, "batch": jnp.minimum(z + 1, 3) * 2 + y}
    return {"seq": x * 2 + c, "batch": jnp.maximum(z - 1, 0) * 2 + y}


def piece_rows(x0, c, z0, y0, rows):
    return pl.ds(pl.multiple_of((2 * x0 + c) * 2496 + z0 * 624 + 320 * y0, 16), rows)


def piece_id(x0, z0, y0):
    return x0 * 8 + z0 * 2 + y0


COLS = ((0, 512), (512, 256))


def entry_barrier():
    x, c, z, y = place()
    bar = pltpu.get_barrier_semaphore()
    for d, cond in (("x", None), ("y", None), ("c", None), ("u", z < 3), ("d", z > 0)):
        when(
            cond,
            lambda d=d: pl.semaphore_signal(bar, 1, device_id=neighbour(d), device_id_type=MESH),
        )
    pl.semaphore_wait(bar, 3 + (z < 3).astype(jnp.int32) + (z > 0).astype(jnp.int32))


class Gather:
    def __init__(self, weights, stage, send_sem, recv_sem, pair_sem):
        self.weights, self.stage = weights, stage
        self.send_sem, self.recv_sem, self.pair_sem = send_sem, recv_sem, pair_sem
        self.sent = []

    def copy(self, t, x0, z0, y0, d, rows, own):
        c = place()[1]
        cols = pl.ds(*COLS[t])
        dst = self.weights.at[piece_rows(x0, c, z0, y0, rows), cols]
        src = self.stage.at[pl.ds(0, rows), cols] if own else dst
        k = piece_id(x0, z0, y0)
        way = {"u": 0, "d": 1, "x": 2 if t else 4, "y": 4 if t else 2, "c": 3}[d]
        return pltpu.make_async_remote_copy(
            src_ref=src,
            dst_ref=dst,
            send_sem=self.send_sem.at[t, k, way],
            recv_sem=(self.pair_sem if d == "c" else self.recv_sem).at[t, k],
            device_id=neighbour(d),
            device_id_type=MESH,
        )

    def send(self, t, x0, z0, y0, ways, own=False, cond=None):
        for d, way_cond in ways:
            whole = both_of(way_cond, cond)
            by_size(y0, whole, lambda rows, d=d: self.copy(t, x0, z0, y0, d, rows, own).start())
            self.sent.append((t, x0, z0, y0, d, own, whole))

    def recv(self, t, x0, z0, y0, cond=None):
        by_size(y0, cond, lambda rows: self.copy(t, x0, z0, y0, "x", rows, False).wait_recv())

    def start(self):
        x, c, z, y = place()
        line = [("u", z < 3), ("d", z > 0), ("c", None)]
        self.send(0, x, z, y, [("x", None), ("y", None)] + line, own=True)
        self.send(1, x, z, y, [("y", None), ("x", None)] + line, own=True)

    def steps(self, g):
        x, c, z, y = place()
        up, down = z < 3, z > 0
        here, there = x == g, x == 1 - g

        def first():
            self.recv(0, g, z, y, cond=there)
            ways = [("u", up), ("d", down), ("y", None), ("c", None)]
            self.send(0, g, z, y, ways, cond=there)
            self.recv(1, g, z, 1 - y, cond=here)
            ways = [("u", up), ("d", down), ("x", None), ("c", None)]
            self.send(1, g, z, 1 - y, ways, cond=here)

        def along(d, sign):
            z0 = z + sign * d
            inside = (z0 >= 0) if sign < 0 else (z0 <= 3)
            relay = ("u", up) if sign < 0 else ("d", down)
            self.recv(0, g, z0, y, cond=inside)
            self.send(0, g, z0, y, [relay, ("y", None), ("c", None)], cond=inside)
            for flip in (0, 1):
                y0 = y if flip == 0 else 1 - y
                self.recv(1, g, z0, y0, cond=both_of(inside, here))
                ways = [relay, ("x", None), ("c", None)]
                self.send(1, g, z0, y0, ways, cond=both_of(inside, here))

        def leaf(z0):
            self.recv(0, g, z0, 1 - y)
            self.send(0, g, z0, 1 - y, [("c", None)])
            for y0 in (0, 1):
                self.recv(1, g, z0, y0, cond=there)
                self.send(1, g, z0, y0, [("c", None)], cond=there)

        out = [first]
        for d in (1, 2, 3):
            for sign in (-1, 1):
                out.append(functools.partial(along, d, sign))
        for z0 in range(4):
            out.append(functools.partial(leaf, z0))
        return out

    def pair_wait(self, g):
        c = place()[1]
        for t in (0, 1):
            for z0 in range(4):
                for y0 in (0, 1):
                    rows = 320 if y0 == 0 else 304
                    ref = self.weights.at[piece_rows(g, 1 - c, z0, y0, rows), pl.ds(*COLS[t])]
                    k = piece_id(g, z0, y0)
                    pltpu.make_async_remote_copy(
                        src_ref=ref,
                        dst_ref=ref,
                        send_sem=self.send_sem.at[t, k, 0],
                        recv_sem=self.pair_sem.at[t, k],
                        device_id=neighbour("c"),
                        device_id_type=MESH,
                    ).wait_recv()

    def finish(self):
        for t, x0, z0, y0, d, own, cond in self.sent:
            by_size(
                y0, cond, lambda rows: self.copy(t, x0, z0, y0, d, rows, own).wait_send()
            )


def dot(first_op, second_op):
    return lax.dot_general(
        first_op, second_op, (((1,), (0,)), ((), ())), preferred_element_type=jnp.float32
    )


def dot_t(first_op, second_op):
    return lax.dot_general(
        first_op, second_op, (((1,), (1,)), ((), ())), preferred_element_type=jnp.float32
    )


def t_dot(first_op, second_op):
    return lax.dot_general(
        first_op, second_op, (((0,), (0,)), ((), ())), preferred_element_type=jnp.float32
    )


def stack_heads(two):
    lane = lax.broadcasted_iota(jnp.int32, two.shape, 1)
    none = jnp.zeros_like(two)
    return jnp.concatenate([jnp.where(lane < 64, two, none), jnp.where(lane < 64, none, two)], axis=0)


def unstack_heads(stacked):
    half = stacked.shape[0] // 2
    lane = lax.broadcasted_iota(jnp.int32, (half, stacked.shape[1]), 1)
    return jnp.where(lane < 64, stacked[:half], stacked[half:])


def attend_row(r, q_ref, k_ref, v_ref, bias, ctx_ref, lse_ref):
    for pair in range(6):
        lanes = pl.ds(pair * 128, 128)
        scores = dot_t(k_ref[r, :, lanes], stack_heads(q_ref[r, :, lanes])) + bias
        top = jnp.max(scores, axis=0, keepdims=True)
        exps = jnp.exp(scores - top)
        total = jnp.sum(exps, axis=0, keepdims=True)
        prob = (exps * (1.0 / total)).astype(jnp.bfloat16)
        ctx_ref[r, :, lanes] = unstack_heads(t_dot(prob, v_ref[r, :, lanes])).astype(jnp.bfloat16)
        lse = top + jnp.log(total)
        lse_ref[r, 2 * pair : 2 * pair + 1, :] = lse[:, :128]
        lse_ref[r, 2 * pair + 1 : 2 * pair + 2, :] = lse[:, 128:]


def norm_rows(z):
    centre = jnp.mean(z, axis=-1, keepdims=True)
    centred = z - centre
    spread = jnp.mean(centred * centred, axis=-1, keepdims=True)
    scale = lax.rsqrt(spread + norm_eps)
    return centred * scale, scale


def norm_back_rows(e, gain, zhat, scale):
    a = e * gain
    mean_a = jnp.mean(a, axis=-1, keepdims=True)
    mean_az = jnp.mean(a * zhat, axis=-1, keepdims=True)
    return (a - mean_a - zhat * mean_az) * scale


def forward_kernel(
    master, values, names, slots, valid, vecs, b_in, out_grad,
    w_out, first_out, pooled_out, q_out, k_out, v_out, valid_out, ctx_out, lse_out,
    zhat_out, scale_out, hidden_out, slope_out, output_out, two_out, vec_out,
    weights, stage, edge, first, pooled, united, q, k, v, valid_all, ctx, lse,
    zhat, scale, hidden, slope, output, two, vec_grad,
    edge_sem, send_sem, recv_sem, pair_sem, kv_send, kv_recv, valid_sem, out_sem,
):
    x, c, z, y = place()
    me = 2 * x + c
    gather = Gather(weights, stage, send_sem, recv_sem, pair_sem)
    entry_barrier()
    edge_copy = pltpu.make_async_remote_copy(
        src_ref=master.at[pl.ds(0, 8)],
        dst_ref=edge,
        send_sem=edge_sem.at[0],
        recv_sem=edge_sem.at[1],
        device_id=neighbour("y"),
        device_id_type=MESH,
    )

    @pl.when(y == 1)
    def _():
        edge_copy.start()
        stage[0:304] = master[8:312].astype(jnp.bfloat16)
        stage[304:320] = jnp.zeros((16, D), jnp.bfloat16)

    @pl.when(y == 0)
    def _():
        stage[0:304] = master[0:304].astype(jnp.bfloat16)
        edge_copy.wait_recv()
        stage[304:320] = jnp.concatenate([master[304:312], edge[...]], axis=0).astype(jnp.bfloat16)

    gather.start()

    def own(rows):
        return pltpu.make_async_copy(
            stage.at[pl.ds(0, rows)], weights.at[piece_rows(x, c, z, y, rows)], edge_sem.at[2]
        )

    by_size(y, None, lambda rows: own(rows).start())

    valid_all[me] = valid[...]

    def valid_copy(where, d, slot):
        return pltpu.make_async_remote_copy(
            src_ref=valid_all.at[where],
            dst_ref=valid_all.at[where],
            send_sem=valid_sem.at[0, slot],
            recv_sem=valid_sem.at[1, slot],
            device_id=neighbour(d),
            device_id_type=MESH,
        )

    valid_copy(me, "x", 0).start()
    valid_copy(me, "c", 1).start()

    for r in range(3):
        rows = pl.ds(r * 128, 128)
        begin, end = slots[rows, 0:1], slots[rows, 1:2]
        slot_id = lax.broadcasted_iota(jnp.int32, (128, NAME_DEV), 1)
        inside = jnp.logical_and(slot_id >= begin, slot_id < end).astype(jnp.float32)
        divisor = jnp.maximum((end - begin).astype(jnp.float32), 1.0)
        summed = dot(inside.astype(jnp.bfloat16), names[r])
        pooled[rows] = (summed / divisor).astype(jnp.bfloat16)

    for step in gather.steps(0):
        step()
    by_size(y, None, lambda rows: own(rows).wait())
    gather.pair_wait(0)

    for j in range(3):
        cols = pl.ds(j * 256, 256)
        tile = values[:, cols].astype(jnp.float32) + dot(pooled[...], weights[4 * D : 5 * D, cols])
        united[:, cols] = tile
        first[:, cols] = tile.astype(jnp.bfloat16)
    here = pl.ds(pl.multiple_of(me * 128, 128), 128)

    def project(base):
        return dot_t(first[...], weights[pl.ds(base, 256)])

    for j in range(3):
        cols = pl.ds(j * 256, 256)
        tile = project(D + j * 256).astype(jnp.bfloat16)
        for r in range(3):
            k[r, here, cols] = tile[r * 128 : (r + 1) * 128]
        tile = (project(2 * D + j * 256) + vecs[1:2, cols]).astype(jnp.bfloat16)
        for r in range(3):
            v[r, here, cols] = tile[r * 128 : (r + 1) * 128]

    def kv_copy(r, which, where, d, slot):
        at = (k if which == 0 else v).at[r, pl.ds(pl.multiple_of(where * 128, 128), 128)]
        return pltpu.make_async_remote_copy(
            src_ref=at,
            dst_ref=at,
            send_sem=kv_send.at[r, which, slot],
            recv_sem=kv_recv.at[r, which, slot],
            device_id=neighbour(d),
            device_id_type=MESH,
        )

    for r in range(3):
        for which in (0, 1):
            kv_copy(r, which, me, "x", 0).start()
            kv_copy(r, which, me, "c", 1).start()
    across, beside, corner = 2 * (1 - x) + c, 2 * x + 1 - c, 2 * (1 - x) + 1 - c
    valid_copy(across, "x", 0).wait_recv()
    valid_copy(across, "c", 2).start()
    for j in range(3):
        cols = pl.ds(j * 256, 256)
        tile = (project(j * 256) + vecs[0:1, cols]).astype(jnp.bfloat16)
        tile = (tile.astype(jnp.float32) * 0.125).astype(jnp.bfloat16)
        for r in range(3):
            q[r, :, cols] = tile[r * 128 : (r + 1) * 128]

    rest = gather.steps(1)
    cut = [rest[:5], rest[5:8], rest[8:]]
    valid_copy(beside, "c", 1).wait_recv()
    valid_copy(corner, "c", 2).wait_recv()
    biases = jnp.concatenate([valid_all[i] for i in range(4)], axis=1)
    bias_cols = jnp.transpose(biases)
    for r in range(3):
        for step in cut[r]:
            step()
        for which in (0, 1):
            kv_copy(r, which, across, "x", 0).wait_recv()
            kv_copy(r, which, across, "c", 2).start()
        for which in (0, 1):
            kv_copy(r, which, beside, "c", 1).wait_recv()
            kv_copy(r, which, corner, "c", 2).wait_recv()
        attend_row(r, q, k, v, bias_cols[:, r : r + 1], ctx, lse)

    outs = []

    def emit(src, dst):
        copy = pltpu.make_async_copy(src, dst, out_sem.at[len(outs)])
        copy.start()
        outs.append(copy)

    emit(first, first_out)
    emit(pooled, pooled_out)
    emit(q, q_out)
    emit(k, k_out)
    emit(v, v_out)
    emit(valid_all, valid_out)
    emit(ctx, ctx_out)
    emit(lse, lse_out)
    gather.pair_wait(1)
    emit(weights, w_out)

    for r in range(3):
        rows = pl.ds(r * 128, 128)
        attn_out = dot(ctx[r], weights[3 * D : 4 * D]) + vecs[2:3]
        hat, rscale = norm_rows(united[rows] + attn_out)
        zhat[rows] = hat
        scale[rows] = jnp.broadcast_to(rscale, (128, 128))
        normed = hat * vecs[3:4] + vecs[4:5]
        united[rows] = normed
        first_low = normed.astype(jnp.bfloat16)
        stage_rows = pl.ds(r * 128, 128)
        output[stage_rows] = first_low
    emit(zhat, zhat_out)
    emit(scale, scale_out)

    def up_tile(j, carry):
        w_tile = weights[pl.ds(pl.multiple_of(5 * D + j * 256, 256), 256)]
        up = dot_t(output[...], w_tile) + b_in[pl.ds(j, 1)]
        below = 0.5 + 0.5 * lax.erf(up * (0.5**0.5))
        density = jnp.exp(-0.5 * up * up) * (1.0 / (2.0 * math.pi) ** 0.5)
        cols = pl.ds(pl.multiple_of(j * 256, 256), 256)
        hidden[:, cols] = (up * below).astype(jnp.bfloat16)
        slope[:, cols] = (below + up * density).astype(jnp.bfloat16)
        return carry

    lax.fori_loop(0, FF // 256, up_tile, 0)
    emit(hidden, hidden_out)
    emit(slope, slope_out)

    grad_gain = jnp.zeros((1, D), jnp.float32)
    grad_shift = jnp.zeros((1, D), jnp.float32)
    for j in range(3):
        cols = pl.ds(j * 256, 256)
        two[:, cols] = (
            dot(hidden[...], weights[5 * D + FF : 5 * D + 2 * FF, cols])
            + vecs[5:6, cols]
            + united[:, cols]
        )
    for r in range(3):
        rows = pl.ds(r * 128, 128)
        hat, rscale = norm_rows(two[rows])
        output[rows] = (hat * vecs[6:7] + vecs[7:8]).astype(jnp.bfloat16)
        e = out_grad[rows].astype(jnp.float32)
        grad_gain += jnp.sum(e * hat, axis=0, keepdims=True)
        grad_shift += jnp.sum(e, axis=0, keepdims=True)
        two[rows] = norm_back_rows(e, vecs[6:7], hat, rscale)
    vec_grad[...] = jnp.zeros((8, D), jnp.float32)
    vec_grad[0:1] = grad_gain
    vec_grad[1:2] = grad_shift
    emit(output, output_out)
    emit(two, two_out)
    emit(vec_grad, vec_out)

    valid_copy(me, "x", 0).wait_send()
    valid_copy(me, "c", 1).wait_send()
    valid_copy(across, "c", 2).wait_send()
    for r in range(3):
        for which in (0, 1):
            kv_copy(r, which, me, "x", 0).wait_send()
            kv_copy(r, which, me, "c", 1).wait_send()
            kv_copy(r, which, across, "c", 2).wait_send()
    gather.finish()
    pl.when(y == 1)(lambda: edge_copy.wait_send())
    for copy in outs:
        copy.wait()


def forward_call(master, values, names, slots, valid, vecs, b_in, out_grad):
    bf, f32 = jnp.bfloat16, jnp.float32
    kept = [
        ((9984, D), bf),
        ((384, D), bf),
        ((384, D), bf),
        ((3, 128, D), bf),
        ((3, 512, D), bf),
        ((3, 512, D), bf),
        ((4, 8, 128), f32),
        ((3, 128, D), bf),
        ((3, 16, 128), f32),
        ((384, D), f32),
        ((384, 128), f32),
        ((384, FF), bf),
        ((384, FF), bf),
        ((384, D), bf),
        ((384, D), f32),
        ((8, D), f32),
    ]
    vmem = pl.BlockSpec(memory_space=pltpu.VMEM)
    held = [pltpu.VMEM(shape, kind) for shape, kind in kept]
    scratch = (
        [held[0], pltpu.VMEM((320, D), bf), pltpu.VMEM((8, D), f32), held[1], held[2]]
        + [pltpu.VMEM((384, D), f32)]
        + held[3:]
    )
    dma = pltpu.SemaphoreType.DMA
    sems = [dma((3,)), dma((2, 16, 5)), dma((2, 16)), dma((2, 16)), dma((3, 2, 3)), dma((3, 2, 3)), dma((2, 3)), dma((16,))]
    return pl.pallas_call(
        forward_kernel,
        out_shape=[jax.ShapeDtypeStruct(shape, kind) for shape, kind in kept],
        in_specs=[vmem] * 8,
        out_specs=[pl.BlockSpec(memory_space=pl.ANY)] * len(kept),
        scratch_shapes=scratch + sems,
        compiler_params=pltpu.CompilerParams(
            collective_id=0, has_side_effects=True, vmem_limit_bytes=58 << 20
        ),
        cost_estimate=pl.CostEstimate(flops=8 * 10**9, bytes_accessed=60 * 10**6, transcendentals=4 * 10**6),
        name="gather_and_forward",
    )(master, values, names, slots, valid, vecs, b_in, out_grad)


def local(
    values,
    names,
    counts,
    valid,
    out_grad,
    master,
    momentum,
    average,
    vectors,
    vector_momentum,
    vector_average,
):
    row_count, row_span, width = values.shape
    token_count = row_count * row_span
    weights = lax.all_gather(master.astype(jnp.bfloat16), ("seq", "batch"), axis=0, tiled=True)
    w_qkv = weights[0 : 3 * D]
    w_attn = weights[3 * D : 4 * D]
    w_unite = weights[4 * D : 5 * D]
    w_in = weights[5 * D : 5 * D + FF]
    w_down = weights[5 * D + FF : 5 * D + 2 * FF]
    bias_q = vectors[0:D]
    bias_v = vectors[D : 2 * D]
    bias_o = vectors[2 * D : 3 * D]
    gain_one = vectors[3 * D : 4 * D]
    shift_one = vectors[4 * D : 5 * D]
    bias_down = vectors[5 * D : 6 * D]
    gain_two = vectors[6 * D : 7 * D]
    shift_two = vectors[7 * D : 8 * D]
    bias_in = vectors[8 * D : 8 * D + FF]
    slot_ends = jnp.cumsum(counts, axis=1)
    slot_starts = slot_ends - counts
    slot_ids = jnp.arange(NAME_DEV, dtype=jnp.int32)
    inside = (slot_ids >= slot_starts[:, :, None]) & (slot_ids < slot_ends[:, :, None])
    summed = jnp.einsum(
        "rtn,rnd->rtd", inside.astype(jnp.bfloat16), names, preferred_element_type=jnp.float32
    )
    divisor = jnp.maximum(counts.astype(jnp.float32), 1.0)[:, :, None]
    pooled = (summed / divisor).astype(jnp.bfloat16).reshape(token_count, D)
    united = values.reshape(token_count, D).astype(jnp.float32) + matmul(pooled, w_unite)
    first = united.astype(jnp.bfloat16)
    projected = matmul_t(first, w_qkv)
    query = (projected[:, 0:D] + bias_q).astype(jnp.bfloat16).reshape(row_count, row_span, D)
    key_proj = projected[:, D : 2 * D].astype(jnp.bfloat16).reshape(row_count, row_span, D)
    value_proj = (
        (projected[:, 2 * D : 3 * D] + bias_v).astype(jnp.bfloat16).reshape(row_count, row_span, D)
    )
    key_all, value_all, mask_all = (
        lax.all_gather(key_proj, "seq", axis=1, tiled=True),
        lax.all_gather(value_proj, "seq", axis=1, tiled=True),
        lax.all_gather(valid.astype(jnp.bfloat16), "seq", axis=1, tiled=True),
    )
    block_rows = math.gcd(row_count, max(1, 512 // row_span))
    block_count = row_count // block_rows

    def blocked(array_in):
        return array_in.reshape((block_count, block_rows) + array_in.shape[1:])

    context, log_total = lax.map(
        attend_block, (blocked(query), blocked(key_all), blocked(value_all), blocked(mask_all))
    )
    context = context.reshape(token_count, D)
    attn_out = matmul(context, w_attn) + bias_o
    normed, norm_one_back = jax.vjp(layer_norm, united + attn_out, gain_one, shift_one)
    lowered = normed.astype(jnp.bfloat16)
    up_proj = matmul_t(lowered, w_in) + bias_in
    activated, gelu_back = jax.vjp(exact_gelu, up_proj)
    hidden = activated.astype(jnp.bfloat16)
    down_proj = matmul(hidden, w_down) + bias_down
    result, norm_two_back = jax.vjp(layer_norm, normed + down_proj, gain_two, shift_two)
    output = result.astype(jnp.bfloat16).reshape(row_count, row_span, D)
    grad_two, grad_gain_two, grad_shift_two = norm_two_back(
        out_grad.reshape(token_count, D).astype(jnp.float32)
    )
    grad_down = grad_two.astype(jnp.bfloat16)
    grad_bias_down = jnp.sum(grad_down.astype(jnp.float32), axis=0)
    grad_w_down = tokens_t(hidden, grad_down)
    grad_hidden = matmul_t(grad_down, w_down)
    grad_up = gelu_back(grad_hidden)[0].astype(jnp.bfloat16)
    grad_bias_in = jnp.sum(grad_up.astype(jnp.float32), axis=0)
    grad_w_in = tokens_t(grad_up, lowered)
    grad_one, grad_gain_one, grad_shift_one = norm_one_back(grad_two + matmul(grad_up, w_in))
    grad_attn = grad_one.astype(jnp.bfloat16)
    grad_bias_o = jnp.sum(grad_attn.astype(jnp.float32), axis=0)
    grad_w_attn = tokens_t(context, grad_attn)
    grad_context = matmul_t(grad_attn, w_attn).astype(jnp.bfloat16).reshape(row_count, row_span, D)
    grad_query, key_terms, value_terms = lax.map(
        attend_back,
        (
            blocked(query),
            blocked(key_all),
            blocked(value_all),
            blocked(mask_all),
            log_total,
            blocked(grad_context),
        ),
    )
    grad_key, grad_value = (
        lax.psum_scatter(
            key_terms.reshape(row_count, -1, D).astype(jnp.bfloat16),
            "seq",
            scatter_dimension=1,
            tiled=True,
        ).astype(jnp.float32),
        lax.psum_scatter(
            value_terms.reshape(row_count, -1, D).astype(jnp.bfloat16),
            "seq",
            scatter_dimension=1,
            tiled=True,
        ).astype(jnp.float32),
    )
    grad_q = grad_query.reshape(token_count, D).astype(jnp.bfloat16)
    grad_k = grad_key.reshape(token_count, D).astype(jnp.bfloat16)
    grad_v = grad_value.reshape(token_count, D).astype(jnp.bfloat16)
    grad_bias_q = jnp.sum(grad_q.astype(jnp.float32), axis=0)
    grad_bias_v = jnp.sum(grad_v.astype(jnp.float32), axis=0)
    grad_qkv = jnp.concatenate([grad_q, grad_k, grad_v], axis=1)
    grad_w_qkv = tokens_t(grad_qkv, first)
    grad_united = grad_one + matmul(grad_qkv, w_qkv)
    grad_unite = grad_united.astype(jnp.bfloat16)
    grad_w_unite = tokens_t(pooled, grad_unite)
    grad_pooled = lax.optimization_barrier(
        matmul_t(grad_unite, w_unite).astype(jnp.bfloat16)
    ).astype(jnp.float32)
    grad_pooled = grad_pooled.reshape(row_count, row_span, D) / divisor
    grad_names = jnp.einsum(
        "rtn,rtd->rnd", inside.astype(jnp.float32), grad_pooled, precision=lax.Precision.HIGHEST
    )
    grad_values = grad_united.reshape(row_count, row_span, D)
    vector_grads = jnp.concatenate(
        [
            grad_bias_q,
            grad_bias_v,
            grad_bias_o,
            grad_gain_one,
            grad_shift_one,
            grad_bias_down,
            grad_gain_two,
            grad_shift_two,
            grad_bias_in,
        ]
    )
    grads = jnp.concatenate([grad_w_qkv, grad_w_attn, grad_w_unite, grad_w_in, grad_w_down], axis=0)
    owned = lax.psum_scatter(grads, ("seq", "batch"), scatter_dimension=0, tiled=True)
    local_squares = jnp.sum(owned * owned)
    vector_total, matrix_squares = lax.psum((vector_grads, local_squares), ("seq", "batch"))
    grad_norm = jnp.sqrt(matrix_squares + jnp.sum(vector_total * vector_total))
    clip_factor = 1.0 / jnp.maximum(grad_norm, 1.0)
    new_master, new_momentum, new_average = apply_update(
        master, momentum, average, owned, clip_factor, step_rate
    )
    new_vectors, new_vector_momentum, new_vector_average = apply_update(
        vectors, vector_momentum, vector_average, vector_total, clip_factor, vector_rate
    )
    return (
        output,
        grad_values,
        grad_names,
        grad_norm,
        new_master,
        new_momentum,
        new_average,
        new_master.astype(jnp.bfloat16),
        new_vectors,
        new_vector_momentum,
        new_vector_average,
    )


def tuned(
    values,
    names,
    counts,
    valid,
    out_grad,
    master,
    momentum,
    average,
    vectors,
    vector_momentum,
    vector_average,
):
    row_count, row_span, width = values.shape
    token_count = row_count * row_span
    slot_ends = jnp.cumsum(counts, axis=1)
    slot_starts = slot_ends - counts
    slots = jnp.stack([slot_starts.reshape(-1), slot_ends.reshape(-1)], axis=1)
    masked = jnp.where(valid > 0, 0.0, big_negative).astype(jnp.float32)
    masked = jnp.concatenate([masked, jnp.zeros((5, 128), jnp.float32)], axis=0)
    vecs = jnp.concatenate([vectors[: 8 * D].reshape(8, D)], axis=0)
    b_in = vectors[8 * D :].reshape(12, 256)
    (weights, first, pooled, q, k, v, valid_all, context, lse, zhat, scale, hidden, slope,
     output, grad_two, vec_grad) = forward_call(
        master, values.reshape(token_count, D), names, slots, masked, vecs, b_in, out_grad.reshape(token_count, D))
    w_qkv = weights[0 : 3 * D]
    w_attn = weights[3 * D : 4 * D]
    w_unite = weights[4 * D : 5 * D]
    w_in = weights[5 * D : 5 * D + FF]
    w_down = weights[5 * D + FF : 5 * D + 2 * FF]
    gain_one = vectors[3 * D : 4 * D]
    shift_one = vectors[4 * D : 5 * D]
    slot_ids = jnp.arange(NAME_DEV, dtype=jnp.int32)
    inside = (slot_ids >= slot_starts[:, :, None]) & (slot_ids < slot_ends[:, :, None])
    divisor = jnp.maximum(counts.astype(jnp.float32), 1.0)[:, :, None]
    context = context.reshape(token_count, D)
    lowered = (zhat * gain_one + shift_one).astype(jnp.bfloat16)
    grad_down = grad_two.astype(jnp.bfloat16)
    grad_bias_down = jnp.sum(grad_down.astype(jnp.float32), axis=0)
    grad_w_down = tokens_t(hidden, grad_down)
    grad_hidden = matmul_t(grad_down, w_down)
    grad_up = (grad_hidden * slope.astype(jnp.float32)).astype(jnp.bfloat16)
    grad_bias_in = jnp.sum(grad_up.astype(jnp.float32), axis=0)
    grad_w_in = tokens_t(grad_up, lowered)
    e_one = grad_two + matmul(grad_up, w_in)
    grad_gain_one = jnp.sum(e_one * zhat, axis=0)
    grad_shift_one = jnp.sum(e_one, axis=0)
    grad_one = norm_back_rows(e_one, gain_one, zhat, scale[:, 0:1])
    grad_attn = grad_one.astype(jnp.bfloat16)
    grad_bias_o = jnp.sum(grad_attn.astype(jnp.float32), axis=0)
    grad_w_attn = tokens_t(context, grad_attn)
    grad_context = matmul_t(grad_attn, w_attn).astype(jnp.bfloat16).reshape(row_count, row_span, D)
    mask_all = (valid_all[:, :3].transpose(1, 0, 2).reshape(3, 512) == 0).astype(jnp.bfloat16)
    grad_query, key_terms, value_terms = attend_back(
        ((q.astype(jnp.float32) * 8).astype(jnp.bfloat16), k, v, mask_all, lse[:, :12], grad_context))
    grad_key, grad_value = (
        lax.psum_scatter(
            key_terms.reshape(row_count, -1, D).astype(jnp.bfloat16),
            "seq",
            scatter_dimension=1,
            tiled=True,
        ).astype(jnp.float32),
        lax.psum_scatter(
            value_terms.reshape(row_count, -1, D).astype(jnp.bfloat16),
            "seq",
            scatter_dimension=1,
            tiled=True,
        ).astype(jnp.float32),
    )
    grad_q = grad_query.reshape(token_count, D).astype(jnp.bfloat16)
    grad_k = grad_key.reshape(token_count, D).astype(jnp.bfloat16)
    grad_v = grad_value.reshape(token_count, D).astype(jnp.bfloat16)
    grad_bias_q = jnp.sum(grad_q.astype(jnp.float32), axis=0)
    grad_bias_v = jnp.sum(grad_v.astype(jnp.float32), axis=0)
    grad_qkv = jnp.concatenate([grad_q, grad_k, grad_v], axis=1)
    grad_w_qkv = tokens_t(grad_qkv, first)
    grad_united = grad_one + matmul(grad_qkv, w_qkv)
    grad_unite = grad_united.astype(jnp.bfloat16)
    grad_w_unite = tokens_t(pooled, grad_unite)
    grad_pooled = lax.optimization_barrier(
        matmul_t(grad_unite, w_unite).astype(jnp.bfloat16)
    ).astype(jnp.float32)
    grad_pooled = grad_pooled.reshape(row_count, row_span, D) / divisor
    grad_names = jnp.einsum(
        "rtn,rtd->rnd", inside.astype(jnp.float32), grad_pooled, precision=lax.Precision.HIGHEST
    )
    grad_values = grad_united.reshape(row_count, row_span, D)
    vector_grads = jnp.concatenate(
        [
            grad_bias_q,
            grad_bias_v,
            grad_bias_o,
            grad_gain_one,
            grad_shift_one,
            grad_bias_down,
            vec_grad[0],
            vec_grad[1],
            grad_bias_in,
        ]
    )
    grads = jnp.concatenate([grad_w_qkv, grad_w_attn, grad_w_unite, grad_w_in, grad_w_down], axis=0)
    owned = lax.psum_scatter(
        grads.astype(jnp.bfloat16), ("seq", "batch"), scatter_dimension=0, tiled=True
    ).astype(jnp.float32)
    local_squares = jnp.sum(owned * owned)
    vector_total, matrix_squares = lax.psum((vector_grads, local_squares), ("seq", "batch"))
    grad_norm = jnp.sqrt(matrix_squares + jnp.sum(vector_total * vector_total))
    clip_factor = 1.0 / jnp.maximum(grad_norm, 1.0)
    new_master, new_momentum, new_average = apply_update(
        master, momentum, average, owned, clip_factor, step_rate
    )
    new_vectors, new_vector_momentum, new_vector_average = apply_update(
        vectors, vector_momentum, vector_average, vector_total, clip_factor, vector_rate
    )
    return (
        output.reshape(values.shape),
        grad_values,
        grad_names,
        grad_norm,
        new_master,
        new_momentum,
        new_average,
        new_master.astype(jnp.bfloat16),
        new_vectors,
        new_vector_momentum,
        new_vector_average,
    )


def solution(mesh):
    chosen = tuned if dict(mesh.shape) == {"seq": 4, "batch": 8} else local
    return jax.shard_map(
        chosen,
        mesh=mesh,
        in_specs=(
            P("batch", "seq", None),
            P("batch", "seq", None),
            P("batch", "seq"),
            P("batch", "seq"),
            P("batch", "seq", None),
            P(("seq", "batch"), None),
            P(("seq", "batch"), None),
            P(("seq", "batch"), None),
            P(),
            P(),
            P(),
        ),
        out_specs=(
            P("batch", "seq", None),
            P("batch", "seq", None),
            P("batch", "seq", None),
            P(),
            P(("seq", "batch"), None),
            P(("seq", "batch"), None),
            P(("seq", "batch"), None),
            P(("seq", "batch"), None),
            P(),
            P(),
            P(),
        ),
        check_vma=False,
    )
```

```python
import functools
import math

import jax
import jax.numpy as jnp
from jax import lax
from jax.experimental import pallas as pl
from jax.experimental.pallas import tpu as pltpu
from jax.sharding import PartitionSpec as P

MESH = pl.DeviceIdType.MESH

D = 768
HEAD = 64
FF = 3072
NAME_DEV = 384


norm_eps = 1e-05
step_rate = 40.0
vector_rate = 240.0
momentum_decay = 0.5
average_decay = 0.5
big_negative = -1e30


def layer_norm(value_in, gain, shift):
    centre = jnp.mean(value_in, axis=-1, keepdims=True)
    centred = value_in - centre
    spread = jnp.mean(centred * centred, axis=-1, keepdims=True)
    return centred * lax.rsqrt(spread + norm_eps) * gain + shift


def exact_gelu(value_in):
    return jax.nn.gelu(value_in, approximate=False)


def matmul(first_op, second_op):
    return jnp.dot(first_op, second_op, preferred_element_type=jnp.float32)


def matmul_t(first_op, second_op):
    return lax.dot_general(
        first_op, second_op, (((1,), (1,)), ((), ())), preferred_element_type=jnp.float32
    )


def tokens_t(first_op, second_op):
    return lax.dot_general(
        first_op, second_op, (((0,), (0,)), ((), ())), preferred_element_type=jnp.float32
    )


def split_heads(array_in):
    return array_in.reshape(array_in.shape[0], array_in.shape[1], array_in.shape[2] // HEAD, HEAD)


def block_scores(query_part, key_part, mask_part):
    scores = jnp.einsum(
        "bqhd,bkhd->bhqk",
        split_heads(query_part),
        split_heads(key_part),
        preferred_element_type=jnp.float32,
    ) * HEAD ** (-0.5)
    return jnp.where(mask_part[:, None, None, :] > 0, scores, big_negative)


def attend_block(pieces):
    query_part, key_part, value_part, mask_part = pieces
    scores = block_scores(query_part, key_part, mask_part)
    top_score = jnp.max(scores, axis=-1, keepdims=True)
    exp_scores = jnp.exp(scores - top_score)
    exp_total = jnp.sum(exp_scores, axis=-1, keepdims=True)
    prob = (exp_scores / exp_total).astype(jnp.bfloat16)
    context = jnp.einsum(
        "bhqk,bkhd->bqhd", prob, split_heads(value_part), preferred_element_type=jnp.float32
    )
    log_total = (top_score + jnp.log(exp_total))[..., 0]
    return (context.reshape(query_part.shape).astype(jnp.bfloat16), log_total)


def attend_back(pieces):
    query_part, key_part, value_part, mask_part, log_total, grad_context = pieces
    scores = block_scores(query_part, key_part, mask_part)
    prob = jnp.exp(scores - log_total[..., None])
    grad_heads = split_heads(grad_context)
    grad_prob = jnp.einsum(
        "bqhd,bkhd->bhqk", grad_heads, split_heads(value_part), preferred_element_type=jnp.float32
    )
    grad_value = jnp.einsum(
        "bhqk,bqhd->bkhd", prob.astype(jnp.bfloat16), grad_heads, preferred_element_type=jnp.float32
    )
    inner = jnp.sum(grad_prob * prob, axis=-1, keepdims=True)
    grad_scores = (prob * (grad_prob - inner)).astype(jnp.bfloat16)
    scale = HEAD ** (-0.5)
    grad_query = (
        jnp.einsum(
            "bhqk,bkhd->bqhd",
            grad_scores,
            split_heads(key_part),
            preferred_element_type=jnp.float32,
        )
        * scale
    )
    grad_key = (
        jnp.einsum(
            "bhqk,bqhd->bkhd",
            grad_scores,
            split_heads(query_part),
            preferred_element_type=jnp.float32,
        )
        * scale
    )
    return (
        grad_query.reshape(query_part.shape),
        grad_key.reshape(key_part.shape),
        grad_value.reshape(value_part.shape),
    )


def apply_update(weight, moment, mean_state, gradient, clip_factor, rate):
    clipped = gradient * clip_factor
    new_moment = momentum_decay * moment + clipped
    new_weight = weight - rate * (clipped + momentum_decay * new_moment)
    new_mean = average_decay * mean_state + (1.0 - average_decay) * new_weight
    return (new_weight, new_moment, new_mean)


def place():
    s = lax.axis_index("seq")
    b = lax.axis_index("batch")
    return s // 2, s % 2, b // 2, b % 2


def when(cond, fn):
    if cond is None:
        fn()
    else:
        pl.when(cond)(fn)


def both_of(first, second):
    if first is None:
        return second
    if second is None:
        return first
    return jnp.logical_and(first, second)


def by_size(y0, cond, fn):
    if isinstance(y0, int):
        when(cond, lambda: fn(320 if y0 == 0 else 304))
    else:
        when(both_of(y0 == 0, cond), lambda: fn(320))
        when(both_of(y0 == 1, cond), lambda: fn(304))


def neighbour(d):
    x, c, z, y = place()
    if d == "x":
        return {"seq": (1 - x) * 2 + c, "batch": z * 2 + y}
    if d == "y":
        return {"seq": x * 2 + c, "batch": z * 2 + 1 - y}
    if d == "c":
        return {"seq": x * 2 + 1 - c, "batch": z * 2 + y}
    if d == "u":
        return {"seq": x * 2 + c, "batch": jnp.minimum(z + 1, 3) * 2 + y}
    return {"seq": x * 2 + c, "batch": jnp.maximum(z - 1, 0) * 2 + y}


def piece_rows(x0, c, z0, y0, rows):
    return pl.ds(pl.multiple_of((2 * x0 + c) * 2496 + z0 * 624 + 320 * y0, 16), rows)


def piece_id(x0, z0, y0):
    return x0 * 8 + z0 * 2 + y0


COLS = ((0, 512), (512, 256))


def entry_barrier():
    x, c, z, y = place()
    bar = pltpu.get_barrier_semaphore()
    for d, cond in (("x", None), ("y", None), ("c", None), ("u", z < 3), ("d", z > 0)):
        when(
            cond,
            lambda d=d: pl.semaphore_signal(bar, 1, device_id=neighbour(d), device_id_type=MESH),
        )
    pl.semaphore_wait(bar, 3 + (z < 3).astype(jnp.int32) + (z > 0).astype(jnp.int32))


class Gather:
    def __init__(self, weights, stage, send_sem, recv_sem, pair_sem):
        self.weights, self.stage = weights, stage
        self.send_sem, self.recv_sem, self.pair_sem = send_sem, recv_sem, pair_sem
        self.sent = []

    def copy(self, t, x0, z0, y0, d, rows, own):
        c = place()[1]
        cols = pl.ds(*COLS[t])
        dst = self.weights.at[piece_rows(x0, c, z0, y0, rows), cols]
        src = self.stage.at[pl.ds(0, rows), cols] if own else dst
        k = piece_id(x0, z0, y0)
        way = {"u": 0, "d": 1, "x": 2 if t else 4, "y": 4 if t else 2, "c": 3}[d]
        return pltpu.make_async_remote_copy(
            src_ref=src,
            dst_ref=dst,
            send_sem=self.send_sem.at[t, k, way],
            recv_sem=(self.pair_sem if d == "c" else self.recv_sem).at[t, k],
            device_id=neighbour(d),
            device_id_type=MESH,
        )

    def send(self, t, x0, z0, y0, ways, own=False, cond=None):
        for d, way_cond in ways:
            whole = both_of(way_cond, cond)
            by_size(y0, whole, lambda rows, d=d: self.copy(t, x0, z0, y0, d, rows, own).start())
            self.sent.append((t, x0, z0, y0, d, own, whole))

    def recv(self, t, x0, z0, y0, cond=None):
        by_size(y0, cond, lambda rows: self.copy(t, x0, z0, y0, "x", rows, False).wait_recv())

    def start(self):
        x, c, z, y = place()
        line = [("u", z < 3), ("d", z > 0), ("c", None)]
        self.send(0, x, z, y, [("x", None), ("y", None)] + line, own=True)
        self.send(1, x, z, y, [("y", None), ("x", None)] + line, own=True)

    def steps(self, g):
        x, c, z, y = place()
        up, down = z < 3, z > 0
        here, there = x == g, x == 1 - g

        def first():
            self.recv(0, g, z, y, cond=there)
            ways = [("u", up), ("d", down), ("y", None), ("c", None)]
            self.send(0, g, z, y, ways, cond=there)
            self.recv(1, g, z, 1 - y, cond=here)
            ways = [("u", up), ("d", down), ("x", None), ("c", None)]
            self.send(1, g, z, 1 - y, ways, cond=here)

        def along(d, sign):
            z0 = z + sign * d
            inside = (z0 >= 0) if sign < 0 else (z0 <= 3)
            relay = ("u", up) if sign < 0 else ("d", down)
            self.recv(0, g, z0, y, cond=inside)
            self.send(0, g, z0, y, [relay, ("y", None), ("c", None)], cond=inside)
            for flip in (0, 1):
                y0 = y if flip == 0 else 1 - y
                self.recv(1, g, z0, y0, cond=both_of(inside, here))
                ways = [relay, ("x", None), ("c", None)]
                self.send(1, g, z0, y0, ways, cond=both_of(inside, here))

        def leaf(z0):
            self.recv(0, g, z0, 1 - y)
            self.send(0, g, z0, 1 - y, [("c", None)])
            for y0 in (0, 1):
                self.recv(1, g, z0, y0, cond=there)
                self.send(1, g, z0, y0, [("c", None)], cond=there)

        out = [first]
        for d in (1, 2, 3):
            for sign in (-1, 1):
                out.append(functools.partial(along, d, sign))
        for z0 in range(4):
            out.append(functools.partial(leaf, z0))
        return out

    def pair_wait(self, g):
        c = place()[1]
        for t in (0, 1):
            for z0 in range(4):
                for y0 in (0, 1):
                    rows = 320 if y0 == 0 else 304
                    ref = self.weights.at[piece_rows(g, 1 - c, z0, y0, rows), pl.ds(*COLS[t])]
                    k = piece_id(g, z0, y0)
                    pltpu.make_async_remote_copy(
                        src_ref=ref,
                        dst_ref=ref,
                        send_sem=self.send_sem.at[t, k, 0],
                        recv_sem=self.pair_sem.at[t, k],
                        device_id=neighbour("c"),
                        device_id_type=MESH,
                    ).wait_recv()

    def finish(self):
        for t, x0, z0, y0, d, own, cond in self.sent:
            by_size(
                y0, cond, lambda rows: self.copy(t, x0, z0, y0, d, rows, own).wait_send()
            )


def dot(first_op, second_op):
    return lax.dot_general(
        first_op, second_op, (((1,), (0,)), ((), ())), preferred_element_type=jnp.float32
    )


def dot_t(first_op, second_op):
    return lax.dot_general(
        first_op, second_op, (((1,), (1,)), ((), ())), preferred_element_type=jnp.float32
    )


def t_dot(first_op, second_op):
    return lax.dot_general(
        first_op, second_op, (((0,), (0,)), ((), ())), preferred_element_type=jnp.float32
    )


def stack_heads(two):
    lane = lax.broadcasted_iota(jnp.int32, two.shape, 1)
    none = jnp.zeros_like(two)
    return jnp.concatenate([jnp.where(lane < 64, two, none), jnp.where(lane < 64, none, two)], axis=0)


def unstack_heads(stacked):
    half = stacked.shape[0] // 2
    lane = lax.broadcasted_iota(jnp.int32, (half, stacked.shape[1]), 1)
    return jnp.where(lane < 64, stacked[:half], stacked[half:])


def attend_row(r, q_ref, k_ref, v_ref, bias, ctx_ref, lse_ref):
    for pair in range(6):
        lanes = pl.ds(pair * 128, 128)
        scores = dot_t(k_ref[r, :, lanes], stack_heads(q_ref[r, :, lanes])) + bias
        top = jnp.max(scores, axis=0, keepdims=True)
        exps = jnp.exp(scores - top)
        total = jnp.sum(exps, axis=0, keepdims=True)
        prob = (exps * (1.0 / total)).astype(jnp.bfloat16)
        ctx_ref[r, :, lanes] = unstack_heads(t_dot(prob, v_ref[r, :, lanes])).astype(jnp.bfloat16)
        lse = top + jnp.log(total)
        lse_ref[r, 2 * pair : 2 * pair + 1, :] = lse[:, :128]
        lse_ref[r, 2 * pair + 1 : 2 * pair + 2, :] = lse[:, 128:]


def norm_rows(z):
    centre = jnp.mean(z, axis=-1, keepdims=True)
    centred = z - centre
    spread = jnp.mean(centred * centred, axis=-1, keepdims=True)
    scale = lax.rsqrt(spread + norm_eps)
    return centred * scale, scale


def norm_back_rows(e, gain, zhat, scale):
    a = e * gain
    mean_a = jnp.mean(a, axis=-1, keepdims=True)
    mean_az = jnp.mean(a * zhat, axis=-1, keepdims=True)
    return (a - mean_a - zhat * mean_az) * scale


def forward_kernel(
    master, values, names, slots, valid, vecs, b_in, out_grad,
    w_out, first_out, pooled_out, q_out, k_out, v_out, valid_out, ctx_out, lse_out,
    zhat_out, scale_out, hidden_out, slope_out, output_out, two_out, vec_out,
    weights, stage, edge, first, pooled, united, q, k, v, valid_all, ctx, lse,
    zhat, scale, hidden, slope, output, two, vec_grad,
    edge_sem, send_sem, recv_sem, pair_sem, kv_send, kv_recv, valid_sem, out_sem,
):
    x, c, z, y = place()
    me = 2 * x + c
    gather = Gather(weights, stage, send_sem, recv_sem, pair_sem)
    entry_barrier()
    edge_copy = pltpu.make_async_remote_copy(
        src_ref=master.at[pl.ds(0, 8)],
        dst_ref=edge,
        send_sem=edge_sem.at[0],
        recv_sem=edge_sem.at[1],
        device_id=neighbour("y"),
        device_id_type=MESH,
    )

    @pl.when(y == 1)
    def _():
        edge_copy.start()
        stage[0:304] = master[8:312].astype(jnp.bfloat16)
        stage[304:320] = jnp.zeros((16, D), jnp.bfloat16)

    @pl.when(y == 0)
    def _():
        stage[0:304] = master[0:304].astype(jnp.bfloat16)
        edge_copy.wait_recv()
        stage[304:320] = jnp.concatenate([master[304:312], edge[...]], axis=0).astype(jnp.bfloat16)

    gather.start()

    def own(rows):
        return pltpu.make_async_copy(
            stage.at[pl.ds(0, rows)], weights.at[piece_rows(x, c, z, y, rows)], edge_sem.at[2]
        )

    by_size(y, None, lambda rows: own(rows).start())

    valid_all[me] = valid[...]

    def valid_copy(where, d, slot):
        return pltpu.make_async_remote_copy(
            src_ref=valid_all.at[where],
            dst_ref=valid_all.at[where],
            send_sem=valid_sem.at[0, slot],
            recv_sem=valid_sem.at[1, slot],
            device_id=neighbour(d),
            device_id_type=MESH,
        )

    valid_copy(me, "x", 0).start()
    valid_copy(me, "c", 1).start()

    for r in range(3):
        rows = pl.ds(r * 128, 128)
        begin, end = slots[rows, 0:1], slots[rows, 1:2]
        slot_id = lax.broadcasted_iota(jnp.int32, (128, NAME_DEV), 1)
        inside = jnp.logical_and(slot_id >= begin, slot_id < end).astype(jnp.float32)
        divisor = jnp.maximum((end - begin).astype(jnp.float32), 1.0)
        summed = dot(inside.astype(jnp.bfloat16), names[r])
        pooled[rows] = (summed / divisor).astype(jnp.bfloat16)

    for step in gather.steps(0):
        step()
    by_size(y, None, lambda rows: own(rows).wait())
    gather.pair_wait(0)

    for j in range(3):
        cols = pl.ds(j * 256, 256)
        tile = values[:, cols].astype(jnp.float32) + dot(pooled[...], weights[4 * D : 5 * D, cols])
        united[:, cols] = tile
        first[:, cols] = tile.astype(jnp.bfloat16)
    here = pl.ds(pl.multiple_of(me * 128, 128), 128)

    def project(base):
        return dot_t(first[...], weights[pl.ds(base, 256)])

    for j in range(3):
        cols = pl.ds(j * 256, 256)
        tile = project(D + j * 256).astype(jnp.bfloat16)
        for r in range(3):
            k[r, here, cols] = tile[r * 128 : (r + 1) * 128]
        tile = (project(2 * D + j * 256) + vecs[1:2, cols]).astype(jnp.bfloat16)
        for r in range(3):
            v[r, here, cols] = tile[r * 128 : (r + 1) * 128]

    def kv_copy(r, which, where, d, slot):
        at = (k if which == 0 else v).at[r, pl.ds(pl.multiple_of(where * 128, 128), 128)]
        return pltpu.make_async_remote_copy(
            src_ref=at,
            dst_ref=at,
            send_sem=kv_send.at[r, which, slot],
            recv_sem=kv_recv.at[r, which, slot],
            device_id=neighbour(d),
            device_id_type=MESH,
        )

    for r in range(3):
        for which in (0, 1):
            kv_copy(r, which, me, "x", 0).start()
            kv_copy(r, which, me, "c", 1).start()
    across, beside, corner = 2 * (1 - x) + c, 2 * x + 1 - c, 2 * (1 - x) + 1 - c
    valid_copy(across, "x", 0).wait_recv()
    valid_copy(across, "c", 2).start()
    for j in range(3):
        cols = pl.ds(j * 256, 256)
        tile = (project(j * 256) + vecs[0:1, cols]).astype(jnp.bfloat16)
        tile = (tile.astype(jnp.float32) * 0.125).astype(jnp.bfloat16)
        for r in range(3):
            q[r, :, cols] = tile[r * 128 : (r + 1) * 128]

    rest = gather.steps(1)
    cut = [rest[:5], rest[5:8], rest[8:]]
    valid_copy(beside, "c", 1).wait_recv()
    valid_copy(corner, "c", 2).wait_recv()
    biases = jnp.concatenate([valid_all[i] for i in range(4)], axis=1)
    bias_cols = jnp.transpose(biases)
    for r in range(3):
        for step in cut[r]:
            step()
        for which in (0, 1):
            kv_copy(r, which, across, "x", 0).wait_recv()
            kv_copy(r, which, across, "c", 2).start()
        for which in (0, 1):
            kv_copy(r, which, beside, "c", 1).wait_recv()
            kv_copy(r, which, corner, "c", 2).wait_recv()
        attend_row(r, q, k, v, bias_cols[:, r : r + 1], ctx, lse)

    outs = []

    def emit(src, dst):
        copy = pltpu.make_async_copy(src, dst, out_sem.at[len(outs)])
        copy.start()
        outs.append(copy)

    emit(first, first_out)
    emit(pooled, pooled_out)
    emit(q, q_out)
    emit(k, k_out)
    emit(v, v_out)
    emit(valid_all, valid_out)
    emit(ctx, ctx_out)
    emit(lse, lse_out)
    gather.pair_wait(1)
    emit(weights, w_out)

    for r in range(3):
        rows = pl.ds(r * 128, 128)
        attn_out = dot(ctx[r], weights[3 * D : 4 * D]) + vecs[2:3]
        hat, rscale = norm_rows(united[rows] + attn_out)
        zhat[rows] = hat
        scale[rows] = jnp.broadcast_to(rscale, (128, 128))
        normed = hat * vecs[3:4] + vecs[4:5]
        united[rows] = normed
        first_low = normed.astype(jnp.bfloat16)
        stage_rows = pl.ds(r * 128, 128)
        output[stage_rows] = first_low
    emit(zhat, zhat_out)
    emit(scale, scale_out)

    def up_tile(j, carry):
        w_tile = weights[pl.ds(pl.multiple_of(5 * D + j * 256, 256), 256)]
        up = dot_t(output[...], w_tile) + b_in[pl.ds(j, 1)]
        below = 0.5 + 0.5 * lax.erf(up * (0.5**0.5))
        density = jnp.exp(-0.5 * up * up) * (1.0 / (2.0 * math.pi) ** 0.5)
        cols = pl.ds(pl.multiple_of(j * 256, 256), 256)
        hidden[:, cols] = (up * below).astype(jnp.bfloat16)
        slope[:, cols] = (below + up * density).astype(jnp.bfloat16)
        return carry

    lax.fori_loop(0, FF // 256, up_tile, 0)
    emit(hidden, hidden_out)
    emit(slope, slope_out)

    grad_gain = jnp.zeros((1, D), jnp.float32)
    grad_shift = jnp.zeros((1, D), jnp.float32)
    for j in range(3):
        cols = pl.ds(j * 256, 256)
        two[:, cols] = (
            dot(hidden[...], weights[5 * D + FF : 5 * D + 2 * FF, cols])
            + vecs[5:6, cols]
            + united[:, cols]
        )
    for r in range(3):
        rows = pl.ds(r * 128, 128)
        hat, rscale = norm_rows(two[rows])
        output[rows] = (hat * vecs[6:7] + vecs[7:8]).astype(jnp.bfloat16)
        e = out_grad[rows].astype(jnp.float32)
        grad_gain += jnp.sum(e * hat, axis=0, keepdims=True)
        grad_shift += jnp.sum(e, axis=0, keepdims=True)
        two[rows] = norm_back_rows(e, vecs[6:7], hat, rscale)
    vec_grad[...] = jnp.zeros((8, D), jnp.float32)
    vec_grad[0:1] = grad_gain
    vec_grad[1:2] = grad_shift
    emit(output, output_out)
    emit(two, two_out)
    emit(vec_grad, vec_out)

    valid_copy(me, "x", 0).wait_send()
    valid_copy(me, "c", 1).wait_send()
    valid_copy(across, "c", 2).wait_send()
    for r in range(3):
        for which in (0, 1):
            kv_copy(r, which, me, "x", 0).wait_send()
            kv_copy(r, which, me, "c", 1).wait_send()
            kv_copy(r, which, across, "c", 2).wait_send()
    gather.finish()
    pl.when(y == 1)(lambda: edge_copy.wait_send())
    for copy in outs:
        copy.wait()


def forward_call(master, values, names, slots, valid, vecs, b_in, out_grad):
    bf, f32 = jnp.bfloat16, jnp.float32
    kept = [
        ((9984, D), bf),
        ((384, D), bf),
        ((384, D), bf),
        ((3, 128, D), bf),
        ((3, 512, D), bf),
        ((3, 512, D), bf),
        ((4, 8, 128), f32),
        ((3, 128, D), bf),
        ((3, 16, 128), f32),
        ((384, D), f32),
        ((384, 128), f32),
        ((384, FF), bf),
        ((384, FF), bf),
        ((384, D), bf),
        ((384, D), f32),
        ((8, D), f32),
    ]
    vmem = pl.BlockSpec(memory_space=pltpu.VMEM)
    held = [pltpu.VMEM(shape, kind) for shape, kind in kept]
    scratch = (
        [held[0], pltpu.VMEM((320, D), bf), pltpu.VMEM((8, D), f32), held[1], held[2]]
        + [pltpu.VMEM((384, D), f32)]
        + held[3:]
    )
    dma = pltpu.SemaphoreType.DMA
    sems = [dma((3,)), dma((2, 16, 5)), dma((2, 16)), dma((2, 16)), dma((3, 2, 3)), dma((3, 2, 3)), dma((2, 3)), dma((16,))]
    return pl.pallas_call(
        forward_kernel,
        out_shape=[jax.ShapeDtypeStruct(shape, kind) for shape, kind in kept],
        in_specs=[vmem] * 8,
        out_specs=[pl.BlockSpec(memory_space=pl.ANY)] * len(kept),
        scratch_shapes=scratch + sems,
        compiler_params=pltpu.CompilerParams(
            collective_id=0, has_side_effects=True, vmem_limit_bytes=58 << 20
        ),
        cost_estimate=pl.CostEstimate(flops=8 * 10**9, bytes_accessed=60 * 10**6, transcendentals=4 * 10**6),
        name="gather_and_forward",
    )(master, values, names, slots, valid, vecs, b_in, out_grad)


def add_rows(dst, dst_rows, src, src_rows, cols, y0):
    def chunk(at, count):
        low = pl.ds(pl.multiple_of(dst_rows + at, 16), count)
        other = pl.ds(pl.multiple_of(src_rows + at, 16), count)
        total = dst[low, cols].astype(jnp.float32) + src[other, cols].astype(jnp.float32)
        dst[low, cols] = total.astype(jnp.bfloat16)

    def body(i, carry):
        chunk(i * 64, 64)
        return carry

    lax.fori_loop(0, 4, body, 0)
    by_size(y0, None, lambda rows: chunk(256, rows - 256))


class Reduce:
    def __init__(self, grads, pair_in, slots_in, pair_send, pair_recv, send_sem, recv_sem):
        self.grads, self.pair_in, self.slots_in = grads, pair_in, slots_in
        self.pair_send, self.pair_recv = pair_send, pair_recv
        self.send_sem, self.recv_sem = send_sem, recv_sem
        self.sent = []
        self.pair_sent = []

    @staticmethod
    def row(x0, c, z0, y0):
        return (2 * x0 + c) * 2496 + z0 * 624 + 320 * y0

    def pair_copy(self, x0, z0, y0):
        c = place()[1]
        rows = 320 if y0 == 0 else 304
        return pltpu.make_async_remote_copy(
            src_ref=self.grads.at[piece_rows(x0, 1 - c, z0, y0, rows)],
            dst_ref=self.pair_in.at[pl.ds(x0 * 2496 + z0 * 624 + y0 * 320, rows)],
            send_sem=self.pair_send.at[x0, z0, y0],
            recv_sem=self.pair_recv.at[x0, z0, y0],
            device_id=neighbour("c"),
            device_id_type=MESH,
        )

    def pair_start(self, pieces, cond):
        def go():
            for x0, z0, y0 in pieces:
                self.pair_copy(x0, z0, y0).start()

        when(cond, go)
        self.pair_sent += [(piece, cond) for piece in pieces]

    def pair_add(self, x0, z0):
        c = place()[1]
        for y0 in (0, 1):
            self.pair_copy(x0, z0, y0).wait_recv()
            add_rows(
                self.grads,
                self.row(x0, c, z0, y0),
                self.pair_in,
                x0 * 2496 + z0 * 624 + y0 * 320,
                slice(None),
                y0,
            )

    def copy(self, t, x0, z0, y0, d, way, slot, rows):
        cols = pl.ds(*COLS[t])
        c = place()[1]
        return pltpu.make_async_remote_copy(
            src_ref=self.grads.at[piece_rows(x0, c, z0, y0, rows), cols],
            dst_ref=self.slots_in.at[pl.ds(pl.multiple_of(slot * 320, 16), rows), cols],
            send_sem=self.send_sem.at[t, way],
            recv_sem=self.recv_sem.at[t, slot],
            device_id=neighbour(d),
            device_id_type=MESH,
        )

    def send(self, t, x0, z0, y0, d, way, slot, cond=None):
        by_size(y0, cond, lambda rows: self.copy(t, x0, z0, y0, d, way, slot, rows).start())
        self.sent.append((t, x0, z0, y0, d, way, slot, cond))

    def take(self, t, x0, z0, y0, slot, cond=None):
        by_size(y0, cond, lambda rows: self.copy(t, x0, z0, y0, "y", 0, slot, rows).wait_recv())
        cols = pl.ds(*COLS[t])
        c = place()[1]
        when(
            cond,
            lambda: add_rows(
                self.grads, self.row(x0, c, z0, y0), self.slots_in, slot * 320, cols, y0
            ),
        )

    def leaf(self, x0, z0, cond=None):
        x, c, z, y = place()
        when(cond, lambda: self.pair_add(x0, z0))
        self.send(0, x0, z0, 1 - y, "y", x0 * 4 + z0, x0 * 4 + z0, cond=cond)
        for y0 in (0, 1):
            far = both_of(x == 1 - x0, cond)
            self.send(1, x0, z0, y0, "x", z0 * 2 + y0, z0 * 2 + y0, cond=far)

    def leaf_take(self, x0, z0):
        x, c, z, y = place()
        self.take(0, x0, z0, y, x0 * 4 + z0)
        for y0 in (0, 1):
            self.take(1, x0, z0, y0, z0 * 2 + y0, cond=x == x0)

    def along(self, x0, dist, sign):
        x, c, z, y = place()
        z0 = z + sign * dist
        inside = (z0 <= 3) if sign > 0 else (z0 >= 0)
        more = both_of(inside, (z > 0) if sign > 0 else (z < 3))
        d = "u" if sign > 0 else "d"
        z0 = jnp.clip(z0, 0, 3)
        there = z0 if sign > 0 or dist > 1 else 4
        kinds = [(0, y, 8 + x0 * 5, 8 + x0 * 4, None)]
        kinds += [(1, y0, 8 + y0 * 5, 8 + y0 * 4, x == x0) for y0 in (0, 1)]
        for t, y0, slot, way, cond in kinds:
            self.take(t, x0, z0, y0, slot + z0, cond=both_of(more, cond))
            self.send(t, x0, z0, y0, d, way + z0, slot + there, cond=both_of(inside, cond))

    def gathered(self, x0):
        x, c, z, y = place()
        kinds = [(0, y, 8 + x0 * 5, None)]
        kinds += [(1, y0, 8 + y0 * 5, x == x0) for y0 in (0, 1)]
        for t, y0, slot, cond in kinds:
            self.take(t, x0, z, y0, slot + z, cond=both_of(z > 0, cond))
            self.take(t, x0, z, y0, slot + 4, cond=both_of(z < 3, cond))
        self.send(0, x0, z, y, "x", 16, 18, cond=x == 1 - x0)
        self.send(1, x0, z, 1 - y, "y", 16, 18, cond=x == x0)

    def final(self, owned):
        x, c, z, y = place()
        for t in (0, 1):
            cols = pl.ds(*COLS[t])
            by_size(y, None, lambda rows: self.copy(t, x, z, y, "y", 0, 18, rows).wait_recv())

            def body(i, carry, cols=cols):
                at = pl.ds(pl.multiple_of(self.row(x, c, z, y) + i * 16, 16), 16)
                other = pl.ds(pl.multiple_of(18 * 320 + i * 16, 16), 16)
                here = pl.ds(pl.multiple_of(i * 16, 16), 16)
                owned[here, cols] = self.grads[at, cols].astype(jnp.float32) + self.slots_in[
                    other, cols
                ].astype(jnp.float32)
                return carry

            lax.fori_loop(0, 20 - y, body, 0)

    def finish(self):
        for piece, cond in self.pair_sent:
            when(cond, lambda piece=piece: self.pair_copy(*piece).wait_send())
        for t, x0, z0, y0, d, way, slot, cond in self.sent:
            by_size(
                y0, cond, lambda rows: self.copy(t, x0, z0, y0, d, way, slot, rows).wait_send()
            )


def attend_row_back(r, q_ref, k_ref, v_ref, gc_ref, bias, lse_ref):
    for pair in range(6):
        lanes = pl.ds(pair * 128, 128)
        q_two = stack_heads(q_ref[r, :, lanes])
        g_two = stack_heads(gc_ref[pl.ds(r * 128, 128), lanes])
        k_two, v_two = k_ref[r, :, lanes], v_ref[r, :, lanes]
        lse = jnp.concatenate(
            [lse_ref[r, 2 * pair : 2 * pair + 1, :], lse_ref[r, 2 * pair + 1 : 2 * pair + 2, :]],
            axis=1,
        )
        prob = jnp.exp(dot_t(k_two, q_two) + bias - lse)
        v_ref[r, :, lanes] = dot(prob.astype(jnp.bfloat16), g_two).astype(jnp.bfloat16)
        grad_prob = dot_t(v_two, g_two)
        inner = jnp.sum(grad_prob * prob, axis=0, keepdims=True)
        grad_scores = (prob * (grad_prob - inner)).astype(jnp.bfloat16)
        k_ref[r, :, lanes] = dot(grad_scores, q_two).astype(jnp.bfloat16)
        grad_q = unstack_heads(t_dot(grad_scores, k_two)) * 0.125
        q_ref[r, :, lanes] = grad_q.astype(jnp.bfloat16)


def wide_barrier():
    s, b = lax.axis_index("seq"), lax.axis_index("batch")
    bar = pltpu.get_barrier_semaphore()
    for i in range(1, 4):
        peer = {"seq": lax.rem(s + i, 4), "batch": b}
        pl.semaphore_signal(bar, 1, device_id=peer, device_id_type=MESH)
    for i in range(1, 8):
        peer = {"seq": s, "batch": lax.rem(b + i, 8)}
        pl.semaphore_signal(bar, 1, device_id=peer, device_id_type=MESH)
    pl.semaphore_wait(bar, 10)


class AllSum:
    def __init__(self, box_seq, box_batch, sems):
        self.boxes, self.sems = (box_seq, box_batch), sems

    def copies(self, stage):
        s, b = lax.axis_index("seq"), lax.axis_index("batch")
        me, size = (s, 4) if stage == 0 else (b, 8)
        box, out = self.boxes[stage], []
        for i in range(1, size):
            there = lax.rem(me + i, size)
            device = {"seq": there, "batch": b} if stage == 0 else {"seq": s, "batch": there}
            out.append(
                pltpu.make_async_remote_copy(
                    src_ref=box.at[me],
                    dst_ref=box.at[me],
                    send_sem=self.sems.at[stage, 0, i],
                    recv_sem=self.sems.at[stage, 1, i],
                    device_id=device,
                    device_id_type=MESH,
                )
            )
        return out

    def start(self, stage, value):
        me = lax.axis_index("seq" if stage == 0 else "batch")
        self.boxes[stage][me] = value
        for copy in self.copies(stage):
            copy.start()

    def total(self, stage):
        for copy in self.copies(stage):
            copy.wait()
        box = self.boxes[stage]
        result = box[0]
        for i in range(1, 4 if stage == 0 else 8):
            result = result + box[i]
        return result


def backward_kernel(
    weights, first_in, pooled_in, q_in, k_in, v_in, ctx_in, zhat_in, scale_in, hidden_in, slope_in,
    two_in, lse, bias_cols, slots_rows, vecs, vec_in,
    values_out, names_out, owned_out, vec_out, square_out,
    w_a, w_b, grads, pair_in, slots_in, first, pooled, q, k, v, ctx, zhat, scale, hidden, slope, two,
    low_a, low_b, low_c, dkv_in, owned, edge, vec_grad, box_seq, box_batch, small_seq, small_batch,
    load_sem, pair_send, pair_recv, send_sem, recv_sem, dkv_send, dkv_recv, edge_sem, sum_sem, small_sem,
    out_sem,
):
    x, c, z, y = place()
    me = 2 * x + c
    f32, bf = jnp.float32, jnp.bfloat16
    loads = {}

    def load(name, src, dst):
        copy = pltpu.make_async_copy(src, dst, load_sem.at[len(loads)])
        copy.start()
        loads[name] = copy

    load("two", two_in, two)
    load("hidden", hidden_in, hidden)
    load("w_down", weights.at[pl.ds(5 * D + FF, FF)], w_a)
    load("slope", slope_in, slope)
    load("w_in", weights.at[pl.ds(5 * D, FF)], w_b.at[pl.ds(0, FF)])
    load("zhat", zhat_in, zhat)
    load("scale", scale_in, scale)
    load("ctx", ctx_in, ctx)
    load("w_o", weights.at[pl.ds(3 * D, D)], w_b.at[pl.ds(FF, D)])
    load("q", q_in, q)
    load("k", k_in, k)
    load("v", v_in, v)
    load("first", first_in, first)
    load("pooled", pooled_in, pooled)
    reduce = Reduce(grads, pair_in, slots_in, pair_send, pair_recv, send_sem, recv_sem)
    wide_barrier()

    def column_sum(value):
        return jnp.sum(value.astype(f32), axis=0, keepdims=True)

    vec_grad[...] = jnp.zeros((16, D), f32)
    loads["two"].wait()
    low_a[...] = two[...].astype(bf)
    vec_grad[5:6] = column_sum(low_a[...])
    loads["hidden"].wait()

    def down_tile(j, carry):
        cols = pl.ds(pl.multiple_of(j * 256, 256), 256)
        rows = pl.ds(pl.multiple_of(5 * D + FF + j * 256, 256), 256)
        grads[rows] = t_dot(hidden[:, cols], low_a[...]).astype(bf)
        return carry

    lax.fori_loop(0, FF // 256, down_tile, 0)
    quarter = [(z0, y0) for z0 in range(4) for y0 in (0, 1)]
    reduce.pair_start([(1, z0, y0) for z0, y0 in quarter], c == 0)
    loads["w_down"].wait()
    loads["slope"].wait()

    def up_tile(j, carry):
        cols = pl.ds(pl.multiple_of(j * 256, 256), 256)
        rows = pl.ds(pl.multiple_of(j * 256, 256), 256)
        tile = (dot_t(low_a[...], w_a[rows]) * slope[:, cols].astype(f32)).astype(bf)
        slope[:, cols] = tile
        here = pl.ds(pl.multiple_of(lax.rem(j, 3) * 256, 256), 256)
        vec_grad[pl.ds(8 + j // 3, 1), here] = column_sum(tile)
        return carry

    lax.fori_loop(0, FF // 256, up_tile, 0)
    load("w_qkv", weights.at[pl.ds(0, 3 * D)], w_a.at[pl.ds(0, 3 * D)])
    load("w_f", weights.at[pl.ds(4 * D, D)], w_a.at[pl.ds(3 * D, D)])
    for z0 in range(4):
        reduce.leaf(1, z0, cond=c == 1)

    loads["w_in"].wait()
    loads["zhat"].wait()
    loads["scale"].wait()
    for j in range(3):
        cols = pl.ds(j * 256, 256)
        two[:, cols] += dot(slope[...], w_b[0:FF, cols])
    grad_gain = jnp.zeros((1, D), f32)
    grad_shift = jnp.zeros((1, D), f32)
    grad_bias = jnp.zeros((1, D), f32)
    for r in range(3):
        rows = pl.ds(r * 128, 128)
        hat, e = zhat[rows], two[rows]
        low_b[rows] = (hat * vecs[3:4] + vecs[4:5]).astype(bf)
        grad_gain += jnp.sum(e * hat, axis=0, keepdims=True)
        grad_shift += jnp.sum(e, axis=0, keepdims=True)
        one = norm_back_rows(e, vecs[3:4], hat, scale[rows, 0:1])
        two[rows] = one
        low_a[rows] = one.astype(bf)
        grad_bias += column_sum(one.astype(bf))
    vec_grad[2:3] = grad_bias
    vec_grad[3:4] = grad_gain
    vec_grad[4:5] = grad_shift
    vec_grad[6:8] = vec_in[0:2]

    def in_tile(j, carry):
        cols = pl.ds(pl.multiple_of(j * 256, 256), 256)
        rows = pl.ds(pl.multiple_of(5 * D + j * 256, 256), 256)
        grads[rows] = t_dot(slope[:, cols], low_b[...]).astype(bf)
        return carry

    lax.fori_loop(0, FF // 256, in_tile, 0)
    reduce.pair_start([(1, z0, y0) for z0, y0 in quarter], c == 1)
    reduce.pair_start([(0, 3, 0), (0, 3, 1), (0, 2, 1)], c == 0)

    loads["ctx"].wait()
    loads["w_o"].wait()
    for j in range(3):
        cols = pl.ds(j * 256, 256)
        grads[3 * D + j * 256 : 3 * D + (j + 1) * 256] = t_dot(ctx[:, cols], low_a[...]).astype(bf)
    reduce.pair_start([(0, 0, 0)], c == 0)
    for j in range(3):
        cols = pl.ds(j * 256, 256)
        low_b[:, cols] = dot_t(low_a[...], w_b[FF + j * 256 : FF + (j + 1) * 256]).astype(bf)
    loads["q"].wait()
    loads["k"].wait()
    loads["v"].wait()

    def block(ref, r, where):
        return ref.at[r, pl.ds(pl.multiple_of(where * 128, 128), 128)]

    def dkv_pair(r, which, x0):
        col = pl.ds((2 * which + x0) * D, D)
        return pltpu.make_async_remote_copy(
            src_ref=block(k if which == 0 else v, r, 2 * x0 + 1 - c),
            dst_ref=hidden.at[pl.ds(r * 128, 128), col],
            send_sem=dkv_send.at[r, which, x0],
            recv_sem=dkv_recv.at[r, which, x0],
            device_id=neighbour("c"),
            device_id_type=MESH,
        )

    def dkv_cross(r, which):
        return pltpu.make_async_remote_copy(
            src_ref=block(k if which == 0 else v, r, 2 * (1 - x) + c),
            dst_ref=dkv_in.at[r, which],
            send_sem=dkv_send.at[r, which, 2],
            recv_sem=dkv_recv.at[r, which, 2],
            device_id=neighbour("x"),
            device_id_type=MESH,
        )

    def dkv_chip(r):
        for which in (0, 1):
            for x0 in (0, 1):
                dkv_pair(r, which, x0).wait_recv()
            for x0 in (0, 1):
                at = pl.ds(pl.multiple_of((2 * x0 + c) * 128, 128), 128)
                ref = k if which == 0 else v
                col = pl.ds((2 * which + x0) * D, D)
                other = hidden[pl.ds(r * 128, 128), col].astype(f32)
                ref[r, at] = (ref[r, at].astype(f32) + other).astype(bf)
            dkv_cross(r, which).start()

    for r in range(3):
        attend_row_back(r, q, k, v, low_b, bias_cols[:, r : r + 1], lse)
        if r == 0:
            for z0 in range(4):
                reduce.leaf(1, z0, cond=c == 0)
        for which in (0, 1):
            for x0 in (0, 1):
                dkv_pair(r, which, x0).start()
        if r > 0:
            dkv_chip(r - 1)
        if r == 1:
            for z0 in range(4):
                reduce.leaf_take(1, z0)
    reduce.along(1, 3, 1)
    reduce.along(1, 3, -1)
    dkv_chip(2)
    reduce.along(1, 2, 1)
    reduce.along(1, 2, -1)

    loads["first"].wait()
    loads["w_qkv"].wait()
    for j in range(3):
        cols = pl.ds(j * 256, 256)
        tile = jnp.concatenate([q[r, :, cols] for r in range(3)], axis=0)
        grads[j * 256 : (j + 1) * 256] = t_dot(tile, first[...]).astype(bf)
        for r in range(3):
            two[pl.ds(r * 128, 128), cols] += dot(q[r], w_a[0:D, cols])
    vec_grad[0:1] = sum(column_sum(q[r]) for r in range(3))
    reduce.along(1, 1, 1)
    reduce.along(1, 1, -1)
    reduce.gathered(1)
    for r in range(3):
        rows = pl.ds(r * 128, 128)
        at = pl.ds(pl.multiple_of(me * 128, 128), 128)
        for which, ref, low in ((0, k, low_a), (1, v, low_c)):
            dkv_cross(r, which).wait_recv()
            low[rows] = (ref[r, at].astype(f32) + dkv_in[r, which].astype(f32)).astype(bf)
    vec_grad[1:2] = column_sum(low_c[...])
    all_sum = AllSum(box_seq, box_batch, sum_sem)
    all_sum.start(0, vec_grad[...])
    for which, low in ((1, low_a), (2, low_c)):
        for j in range(3):
            cols = pl.ds(j * 256, 256)
            base = which * D + j * 256
            grads[base : base + 256] = t_dot(low[:, cols], first[...]).astype(bf)
    reduce.pair_start([(0, z0, y0) for z0, y0 in quarter], c == 1)
    loads["w_f"].wait()
    for j in range(3):
        cols = pl.ds(j * 256, 256)
        two[:, cols] += dot(low_a[...], w_a[D : 2 * D, cols]) + dot(low_c[...], w_a[2 * D : 3 * D, cols])
    outs = []

    def emit(src, dst):
        copy = pltpu.make_async_copy(src, dst, out_sem.at[len(outs)])
        copy.start()
        outs.append(copy)

    emit(two, values_out)
    low_b[...] = two[...].astype(bf)
    loads["pooled"].wait()
    for j in range(3):
        cols = pl.ds(j * 256, 256)
        grads[4 * D + j * 256 : 4 * D + (j + 1) * 256] = t_dot(pooled[:, cols], low_b[...]).astype(bf)
    reduce.pair_start([(0, 0, 1), (0, 1, 0), (0, 1, 1), (0, 2, 0)], c == 0)
    vec_seq = all_sum.total(0)
    all_sum.start(1, vec_seq)
    for z0 in range(4):
        reduce.leaf(0, z0)

    for j in range(3):
        cols = pl.ds(j * 256, 256)
        low_a[:, cols] = dot_t(low_b[...], w_a[3 * D + j * 256 : 3 * D + (j + 1) * 256]).astype(bf)
    slot_id = lax.broadcasted_iota(jnp.int32, (NAME_DEV, 128), 0)
    for r in range(3):
        begin, end = slots_rows[r : r + 1], slots_rows[3 + r : 4 + r]
        inside = jnp.logical_and(slot_id >= begin, slot_id < end)
        inside = inside.astype(f32)
        share = jnp.sum(inside * (end - begin).astype(f32), axis=1, keepdims=True)
        spread = dot(inside.astype(bf), low_a[pl.ds(r * 128, 128)])
        if r > 0:
            outs[-1].wait()
            outs.pop()
        zhat[...] = spread / jnp.maximum(share, 1.0)
        copy = pltpu.make_async_copy(zhat, names_out.at[r], out_sem.at[8 + r])
        copy.start()
        outs.append(copy)

    for z0 in range(4):
        reduce.leaf_take(0, z0)
    for dist in (3, 2, 1):
        reduce.along(0, dist, 1)
        reduce.along(0, dist, -1)
    reduce.gathered(0)
    vec_out[...] = all_sum.total(1)
    reduce.final(owned)

    edge_copy = pltpu.make_async_remote_copy(
        src_ref=owned.at[pl.ds(312, 8)],
        dst_ref=edge,
        send_sem=edge_sem.at[0],
        recv_sem=edge_sem.at[1],
        device_id=neighbour("y"),
        device_id_type=MESH,
    )

    @pl.when(y == 0)
    def _():
        edge_copy.start()
        owned_out[...] = owned[0:312]

    @pl.when(y == 1)
    def _():
        owned_out[8:312] = owned[0:304]
        edge_copy.wait_recv()
        owned_out[0:8] = edge[...]

    squares = jnp.sum(owned_out[...] * owned_out[...])
    small = AllSum(small_seq, small_batch, small_sem)
    small.start(0, jnp.full((8, 128), squares, f32))
    part = small.total(0)
    small.start(1, part)
    square_out[...] = small.total(1)

    pl.when(y == 0)(lambda: edge_copy.wait_send())
    for r in range(3):
        for which in (0, 1):
            for x0 in (0, 1):
                dkv_pair(r, which, x0).wait_send()
            dkv_cross(r, which).wait_send()
    reduce.finish()
    for copy in outs:
        copy.wait()


def backward_call(weights, first, pooled, q, k, v, ctx, zhat, scale, hidden, slope, two, lse, bias_cols, slots_rows, vecs, vec_grad):
    bf, f32 = jnp.bfloat16, jnp.float32
    vmem = pl.BlockSpec(memory_space=pltpu.VMEM)
    hbm = pl.BlockSpec(memory_space=pl.ANY)
    dma = pltpu.SemaphoreType.DMA
    low = pltpu.VMEM((384, D), bf)
    wide = pltpu.VMEM((384, D), f32)
    scratch = [
        pltpu.VMEM((FF, D), bf),
        pltpu.VMEM((FF + D, D), bf),
        pltpu.VMEM((9984, D), bf),
        pltpu.VMEM((4992, D), bf),
        pltpu.VMEM((19 * 320, D), bf),
        low,
        low,
        pltpu.VMEM((3, 128, D), bf),
        pltpu.VMEM((3, 512, D), bf),
        pltpu.VMEM((3, 512, D), bf),
        low,
        wide,
        pltpu.VMEM((384, 128), f32),
        pltpu.VMEM((384, FF), bf),
        pltpu.VMEM((384, FF), bf),
        wide,
        low,
        low,
        low,
        pltpu.VMEM((3, 2, 128, D), bf),
        pltpu.VMEM((320, D), f32),
        pltpu.VMEM((8, D), f32),
        pltpu.VMEM((16, D), f32),
        pltpu.VMEM((4, 16, D), f32),
        pltpu.VMEM((8, 16, D), f32),
        pltpu.VMEM((4, 8, 128), f32),
        pltpu.VMEM((8, 8, 128), f32),
        dma((16,)),
        dma((2, 4, 2)),
        dma((2, 4, 2)),
        dma((2, 17)),
        dma((2, 19)),
        dma((3, 2, 3)),
        dma((3, 2, 3)),
        dma((2,)),
        dma((2, 2, 8)),
        dma((2, 2, 8)),
        dma((12,)),
    ]
    return pl.pallas_call(
        backward_kernel,
        out_shape=[
            jax.ShapeDtypeStruct((384, D), f32),
            jax.ShapeDtypeStruct((3, NAME_DEV, D), f32),
            jax.ShapeDtypeStruct((312, D), f32),
            jax.ShapeDtypeStruct((16, D), f32),
            jax.ShapeDtypeStruct((8, 128), f32),
        ],
        in_specs=[hbm] * 12 + [vmem] * 5,
        out_specs=[hbm, hbm, vmem, vmem, vmem],
        scratch_shapes=scratch,
        compiler_params=pltpu.CompilerParams(
            collective_id=1, has_side_effects=True, vmem_limit_bytes=63 << 20
        ),
        cost_estimate=pl.CostEstimate(flops=16 * 10**9, bytes_accessed=60 * 10**6, transcendentals=3 * 10**6),
        name="backward_and_reduce",
    )(weights, first, pooled, q, k, v, ctx, zhat, scale, hidden, slope, two, lse, bias_cols, slots_rows, vecs, vec_grad)


def local(
    values,
    names,
    counts,
    valid,
    out_grad,
    master,
    momentum,
    average,
    vectors,
    vector_momentum,
    vector_average,
):
    row_count, row_span, width = values.shape
    token_count = row_count * row_span
    weights = lax.all_gather(master.astype(jnp.bfloat16), ("seq", "batch"), axis=0, tiled=True)
    w_qkv = weights[0 : 3 * D]
    w_attn = weights[3 * D : 4 * D]
    w_unite = weights[4 * D : 5 * D]
    w_in = weights[5 * D : 5 * D + FF]
    w_down = weights[5 * D + FF : 5 * D + 2 * FF]
    bias_q = vectors[0:D]
    bias_v = vectors[D : 2 * D]
    bias_o = vectors[2 * D : 3 * D]
    gain_one = vectors[3 * D : 4 * D]
    shift_one = vectors[4 * D : 5 * D]
    bias_down = vectors[5 * D : 6 * D]
    gain_two = vectors[6 * D : 7 * D]
    shift_two = vectors[7 * D : 8 * D]
    bias_in = vectors[8 * D : 8 * D + FF]
    slot_ends = jnp.cumsum(counts, axis=1)
    slot_starts = slot_ends - counts
    slot_ids = jnp.arange(NAME_DEV, dtype=jnp.int32)
    inside = (slot_ids >= slot_starts[:, :, None]) & (slot_ids < slot_ends[:, :, None])
    summed = jnp.einsum(
        "rtn,rnd->rtd", inside.astype(jnp.bfloat16), names, preferred_element_type=jnp.float32
    )
    divisor = jnp.maximum(counts.astype(jnp.float32), 1.0)[:, :, None]
    pooled = (summed / divisor).astype(jnp.bfloat16).reshape(token_count, D)
    united = values.reshape(token_count, D).astype(jnp.float32) + matmul(pooled, w_unite)
    first = united.astype(jnp.bfloat16)
    projected = matmul_t(first, w_qkv)
    query = (projected[:, 0:D] + bias_q).astype(jnp.bfloat16).reshape(row_count, row_span, D)
    key_proj = projected[:, D : 2 * D].astype(jnp.bfloat16).reshape(row_count, row_span, D)
    value_proj = (
        (projected[:, 2 * D : 3 * D] + bias_v).astype(jnp.bfloat16).reshape(row_count, row_span, D)
    )
    key_all, value_all, mask_all = (
        lax.all_gather(key_proj, "seq", axis=1, tiled=True),
        lax.all_gather(value_proj, "seq", axis=1, tiled=True),
        lax.all_gather(valid.astype(jnp.bfloat16), "seq", axis=1, tiled=True),
    )
    block_rows = math.gcd(row_count, max(1, 512 // row_span))
    block_count = row_count // block_rows

    def blocked(array_in):
        return array_in.reshape((block_count, block_rows) + array_in.shape[1:])

    context, log_total = lax.map(
        attend_block, (blocked(query), blocked(key_all), blocked(value_all), blocked(mask_all))
    )
    context = context.reshape(token_count, D)
    attn_out = matmul(context, w_attn) + bias_o
    normed, norm_one_back = jax.vjp(layer_norm, united + attn_out, gain_one, shift_one)
    lowered = normed.astype(jnp.bfloat16)
    up_proj = matmul_t(lowered, w_in) + bias_in
    activated, gelu_back = jax.vjp(exact_gelu, up_proj)
    hidden = activated.astype(jnp.bfloat16)
    down_proj = matmul(hidden, w_down) + bias_down
    result, norm_two_back = jax.vjp(layer_norm, normed + down_proj, gain_two, shift_two)
    output = result.astype(jnp.bfloat16).reshape(row_count, row_span, D)
    grad_two, grad_gain_two, grad_shift_two = norm_two_back(
        out_grad.reshape(token_count, D).astype(jnp.float32)
    )
    grad_down = grad_two.astype(jnp.bfloat16)
    grad_bias_down = jnp.sum(grad_down.astype(jnp.float32), axis=0)
    grad_w_down = tokens_t(hidden, grad_down)
    grad_hidden = matmul_t(grad_down, w_down)
    grad_up = gelu_back(grad_hidden)[0].astype(jnp.bfloat16)
    grad_bias_in = jnp.sum(grad_up.astype(jnp.float32), axis=0)
    grad_w_in = tokens_t(grad_up, lowered)
    grad_one, grad_gain_one, grad_shift_one = norm_one_back(grad_two + matmul(grad_up, w_in))
    grad_attn = grad_one.astype(jnp.bfloat16)
    grad_bias_o = jnp.sum(grad_attn.astype(jnp.float32), axis=0)
    grad_w_attn = tokens_t(context, grad_attn)
    grad_context = matmul_t(grad_attn, w_attn).astype(jnp.bfloat16).reshape(row_count, row_span, D)
    grad_query, key_terms, value_terms = lax.map(
        attend_back,
        (
            blocked(query),
            blocked(key_all),
            blocked(value_all),
            blocked(mask_all),
            log_total,
            blocked(grad_context),
        ),
    )
    grad_key, grad_value = (
        lax.psum_scatter(
            key_terms.reshape(row_count, -1, D).astype(jnp.bfloat16),
            "seq",
            scatter_dimension=1,
            tiled=True,
        ).astype(jnp.float32),
        lax.psum_scatter(
            value_terms.reshape(row_count, -1, D).astype(jnp.bfloat16),
            "seq",
            scatter_dimension=1,
            tiled=True,
        ).astype(jnp.float32),
    )
    grad_q = grad_query.reshape(token_count, D).astype(jnp.bfloat16)
    grad_k = grad_key.reshape(token_count, D).astype(jnp.bfloat16)
    grad_v = grad_value.reshape(token_count, D).astype(jnp.bfloat16)
    grad_bias_q = jnp.sum(grad_q.astype(jnp.float32), axis=0)
    grad_bias_v = jnp.sum(grad_v.astype(jnp.float32), axis=0)
    grad_qkv = jnp.concatenate([grad_q, grad_k, grad_v], axis=1)
    grad_w_qkv = tokens_t(grad_qkv, first)
    grad_united = grad_one + matmul(grad_qkv, w_qkv)
    grad_unite = grad_united.astype(jnp.bfloat16)
    grad_w_unite = tokens_t(pooled, grad_unite)
    grad_pooled = lax.optimization_barrier(
        matmul_t(grad_unite, w_unite).astype(jnp.bfloat16)
    ).astype(jnp.float32)
    grad_pooled = grad_pooled.reshape(row_count, row_span, D) / divisor
    grad_names = jnp.einsum(
        "rtn,rtd->rnd", inside.astype(jnp.float32), grad_pooled, precision=lax.Precision.HIGHEST
    )
    grad_values = grad_united.reshape(row_count, row_span, D)
    vector_grads = jnp.concatenate(
        [
            grad_bias_q,
            grad_bias_v,
            grad_bias_o,
            grad_gain_one,
            grad_shift_one,
            grad_bias_down,
            grad_gain_two,
            grad_shift_two,
            grad_bias_in,
        ]
    )
    grads = jnp.concatenate([grad_w_qkv, grad_w_attn, grad_w_unite, grad_w_in, grad_w_down], axis=0)
    owned = lax.psum_scatter(grads, ("seq", "batch"), scatter_dimension=0, tiled=True)
    local_squares = jnp.sum(owned * owned)
    vector_total, matrix_squares = lax.psum((vector_grads, local_squares), ("seq", "batch"))
    grad_norm = jnp.sqrt(matrix_squares + jnp.sum(vector_total * vector_total))
    clip_factor = 1.0 / jnp.maximum(grad_norm, 1.0)
    new_master, new_momentum, new_average = apply_update(
        master, momentum, average, owned, clip_factor, step_rate
    )
    new_vectors, new_vector_momentum, new_vector_average = apply_update(
        vectors, vector_momentum, vector_average, vector_total, clip_factor, vector_rate
    )
    return (
        output,
        grad_values,
        grad_names,
        grad_norm,
        new_master,
        new_momentum,
        new_average,
        new_master.astype(jnp.bfloat16),
        new_vectors,
        new_vector_momentum,
        new_vector_average,
    )


def tuned(
    values,
    names,
    counts,
    valid,
    out_grad,
    master,
    momentum,
    average,
    vectors,
    vector_momentum,
    vector_average,
):
    row_count, row_span, width = values.shape
    token_count = row_count * row_span
    slot_ends = jnp.cumsum(counts, axis=1)
    slot_starts = slot_ends - counts
    slots = jnp.stack([slot_starts.reshape(-1), slot_ends.reshape(-1)], axis=1)
    masked = jnp.where(valid > 0, 0.0, big_negative).astype(jnp.float32)
    masked = jnp.concatenate([masked, jnp.zeros((5, 128), jnp.float32)], axis=0)
    vecs = jnp.concatenate([vectors[: 8 * D].reshape(8, D)], axis=0)
    b_in = vectors[8 * D :].reshape(12, 256)
    (weights, first, pooled, q, k, v, valid_all, context, lse, zhat, scale, hidden, slope,
     output, grad_two, vec_grad) = forward_call(
        master, values.reshape(token_count, D), names, slots, masked, vecs, b_in, out_grad.reshape(token_count, D))
    bias_cols = jnp.transpose(valid_all, (0, 2, 1)).reshape(512, 8)
    slots_rows = jnp.concatenate([slot_starts, slot_ends, slot_ends[:2] * 0], axis=0)
    grad_values, grad_names, owned, vec_total, squares = backward_call(
        weights, first, pooled, q, k, v, context.reshape(token_count, D), zhat, scale, hidden, slope, grad_two, lse, bias_cols, slots_rows, vecs, vec_grad)
    grad_values = grad_values.reshape(values.shape)
    vector_total = vec_total[:12].reshape(-1)
    matrix_squares = squares[0, 0]
    grad_norm = jnp.sqrt(matrix_squares + jnp.sum(vector_total * vector_total))
    clip_factor = 1.0 / jnp.maximum(grad_norm, 1.0)
    new_master, new_momentum, new_average = apply_update(
        master, momentum, average, owned, clip_factor, step_rate
    )
    new_vectors, new_vector_momentum, new_vector_average = apply_update(
        vectors, vector_momentum, vector_average, vector_total, clip_factor, vector_rate
    )
    return (
        output.reshape(values.shape),
        grad_values,
        grad_names,
        grad_norm,
        new_master,
        new_momentum,
        new_average,
        new_master.astype(jnp.bfloat16),
        new_vectors,
        new_vector_momentum,
        new_vector_average,
    )


def solution(mesh):
    chosen = tuned if dict(mesh.shape) == {"seq": 4, "batch": 8} else local
    return jax.shard_map(
        chosen,
        mesh=mesh,
        in_specs=(
            P("batch", "seq", None),
            P("batch", "seq", None),
            P("batch", "seq"),
            P("batch", "seq"),
            P("batch", "seq", None),
            P(("seq", "batch"), None),
            P(("seq", "batch"), None),
            P(("seq", "batch"), None),
            P(),
            P(),
            P(),
        ),
        out_specs=(
            P("batch", "seq", None),
            P("batch", "seq", None),
            P("batch", "seq", None),
            P(),
            P(("seq", "batch"), None),
            P(("seq", "batch"), None),
            P(("seq", "batch"), None),
            P(("seq", "batch"), None),
            P(),
            P(),
            P(),
        ),
        check_vma=False,
    )
```
